32 devices in a mesh: band: 4 (over x, core), grid: 8 (over z, y).
Axes of the slice: x: 2, y: 2, z: 4, core: 2. Of those that a mesh axis runs over, the one named last changes fastest.
Arguments:
- orbitals: float32 [96, 16, 16, 512], P('grid', None, None, 'band'), may hold values from -24 to 24
- potential: float32 [96, 16, 16], P('grid'), may hold values from -3 to -1
- projectors: float32 [32, 8, 13, 256], P('grid'), may hold values from -0.109375 to 0.109375
- atom_planes: int32 [32, 13], P('grid'), may hold values from 0 to 23, as said below
- kb_energy: float32 [8], replicated, may hold values from 1 to 4
Outputs:
- filtered: float32 [96, 16, 16, 512], P('grid', None, None, 'band')
- correlation_gram: float32 [512, 512], P('band')
The draws below stay inside these ranges and needn't reach their ends.
Inputs may be any that keep to these rules, and one draw needn't show every extreme that they name: `atom_planes`: each atom's row holds 13 consecutive plane numbers; the first atom starts at plane 0 and the last atom at plane 12 - 1.
All inputs are finite; a program needn't handle non-finite values.
Results may differ from the reference program's by a relative error of at most 0.0003.
Values sent between devices are 32-bit elements; how exact they have to be, the bound alone decides.
No kernel may reach another device: no remote copies, remote signals or barrier semaphores. Data moves between devices by JAX's collectives and lax.ppermute only.
A program may use at most 128 MiB of HBM per device.

```python
import jax
import jax.numpy as jnp
from jax import lax

NORB = 512
CX = 12
NY = 16
NZ = 16
ATOM_DEV = 4
NPJ = 8
NBLK = 13
DEGREE = 4
NX = 96
NATOM = 32
CELLS = 24576


def draw_atom_planes(key, part):
    offsets = jax.random.randint(key, (NATOM,), 0, CX, dtype=jnp.int32)
    offsets = offsets.at[0].set(0).at[NATOM - 1].set(CX - 1)
    return offsets[:, None] + jnp.arange(NBLK, dtype=jnp.int32)[None, :]


def block_scale(own_key, extent, shards, least, top_value):
    factor_of, own = 1.0, jax.random.fold_in(own_key, 6)
    for dim, parts in shards:
        draws = jnp.exp(jax.random.uniform(jax.random.fold_in(own, dim), (parts,), jnp.float32, least / len(shards), top_value / len(shards)))
        factor_of = factor_of * jnp.repeat(draws, extent[dim] // parts).reshape([-1 if axis == dim else 1 for axis in range(len(extent))])
    return factor_of


def noise(rng, dims, spread, limit, cuts=(), kind=jnp.bfloat16):
    array = spread * jax.random.normal(rng, dims, jnp.float32)
    if cuts:
        array = array * block_scale(rng, dims, cuts, -0.22, 0.18)
    return jnp.clip(array, -limit, limit).astype(kind)


def setup_inputs(seed: int = 0) -> dict:
    streams_of = jax.random.split(jax.random.key(seed), 6)
    orbitals = noise(streams_of[0], (NX, NY, NZ, NORB), 4.0, 24.0, ((0, 8), (3, 4)), jnp.float32)
    potential = jnp.clip(-3.0 + 2.0 * jax.random.uniform(streams_of[1], (NX, NY, NZ), jnp.float32) ** block_scale(streams_of[1], (NX, NY, NZ), ((0, 8),), -0.2, 0.2), -3.0, -1.0)
    projectors = noise(streams_of[2], (NATOM, NPJ, NBLK, NY * NZ), (NBLK * NY * NZ) ** -0.5, 0.109375, ((0, 8),), jnp.float32)
    atom_planes = draw_atom_planes(jax.random.fold_in(streams_of[5], 71), 0)
    kb_energy = jnp.clip(jax.random.uniform(streams_of[4], (NPJ,), jnp.float32, 1.0, 4.0), 1.0, 4.0)
    return dict(orbitals=orbitals, potential=potential, projectors=projectors, atom_planes=atom_planes, kb_energy=kb_energy)


WEIGHTS = (-5369.0 / 1800.0, 12.0 / 7.0, -15.0 / 56.0, 10.0 / 189.0, -1.0 / 112.0, 2.0 / 1925.0, -1.0 / 16632.0)
LOWER = -4.0
CUTOFF = 1.0
UPPER = 16.0
PRECISE = lax.Precision.HIGHEST


def filter_terms(degree):
    half_span = (UPPER - CUTOFF) / 2.0
    middle = (UPPER + CUTOFF) / 2.0
    sigma_now = half_span / (LOWER - middle)
    sigma_first = sigma_now
    scales = [sigma_now / half_span]
    recall = [0.0]
    for level in range(1, degree):
        sigma_next = 1.0 / (2.0 / sigma_first - sigma_now)
        scales.append(2.0 * sigma_next / half_span)
        recall.append(sigma_now * sigma_next)
        sigma_now = sigma_next
    return middle, scales, recall


def second_roll(values, along):
    summed = WEIGHTS[0] * values
    for reach in range(1, 7):
        summed = summed + WEIGHTS[reach] * (jnp.roll(values, reach, along) + jnp.roll(values, -reach, along))
    return summed


def nonlocal_term(values, projectors, atom_planes, kb_energy):
    offsets = (jnp.arange(NATOM, dtype=jnp.int32) // ATOM_DEV) * CX - 6

    def add_atom(accum, atom_data):
        chi_rows, rows_here, offset = atom_data
        plane_ids = ((offset + rows_here) % NX).astype(jnp.int32)
        gathered = values[plane_ids].reshape(-1, NORB)
        chi_flat = chi_rows.reshape(NPJ, -1)
        correlation = jnp.dot(chi_flat, gathered, precision=PRECISE) * kb_energy[:, None]
        contrib = lax.dot_general(chi_flat, correlation, (((0,), (0,)), ((), ())), precision=PRECISE)
        return accum.at[plane_ids].add(contrib.reshape(NBLK, NY, NZ, NORB)), None

    accum, unused = lax.scan(add_atom, jnp.zeros_like(values), (projectors, atom_planes, offsets))
    return accum


def hamiltonian(values, potential, projectors, atom_planes, kb_energy):
    lap = second_roll(values, 0) + second_roll(values, 1) + second_roll(values, 2)
    local_part = -0.5 * lap + potential[..., None] * values
    return local_part + nonlocal_term(values, projectors, atom_planes, kb_energy)


def reference(orbitals, potential, projectors, atom_planes, kb_energy):
    middle, scales, recall = filter_terms(DEGREE)
    previous = orbitals
    current = orbitals
    for level in range(DEGREE):
        applied = hamiltonian(current, potential, projectors, atom_planes, kb_energy)
        result = scales[level] * (applied - middle * current)
        if level > 0:
            result = result - recall[level] * previous
        previous = current
        current = result
    flattened = current.reshape(-1, NORB)
    correlation_gram = lax.dot_general(flattened, flattened, (((0,), (0,)), ((), ())), precision=PRECISE) * (1.0 / CELLS)
    return current, correlation_gram
```

```python
import functools

import jax
import jax.numpy as jnp
import ml_dtypes
import numpy as np
from jax import lax
from jax.experimental import pallas as pl
from jax.experimental.pallas import tpu as pltpu
from jax.sharding import PartitionSpec as P

DEGREE = 4
REACH = 6
LANES = 128
QUARTER = 32

WEIGHTS = (
    -5369.0 / 1800.0,
    12.0 / 7.0,
    -15.0 / 56.0,
    10.0 / 189.0,
    -1.0 / 112.0,
    2.0 / 1925.0,
    -1.0 / 16632.0,
)
LOWER = -4.0
CUTOFF = 1.0
UPPER = 16.0
F32 = jnp.float32
BF16 = jnp.bfloat16


def filter_terms(degree):
    half_span = (UPPER - CUTOFF) / 2.0
    middle = (UPPER + CUTOFF) / 2.0
    sigma_now = half_span / (LOWER - middle)
    sigma_first = sigma_now
    scales = [sigma_now / half_span]
    recall = [0.0]
    for level in range(1, degree):
        sigma_next = 1.0 / (2.0 / sigma_first - sigma_now)
        scales.append(2.0 * sigma_next / half_span)
        recall.append(sigma_now * sigma_next)
        sigma_now = sigma_next
    return (middle, scales, recall)


def plane_matrix(ny, nz):
    def ring(n):
        m = np.zeros((n, n))
        for i in range(n):
            m[i, i] += WEIGHTS[0]
            for r in range(1, REACH + 1):
                m[i, (i + r) % n] += WEIGHTS[r]
                m[i, (i - r) % n] += WEIGHTS[r]
        return m

    full = -0.5 * (np.kron(ring(ny), np.eye(nz)) + np.kron(np.eye(ny), ring(nz)))
    high = full.astype(ml_dtypes.bfloat16)
    low = (full - high.astype(np.float64)).astype(ml_dtypes.bfloat16)
    return high, low


def halves(value):
    high = value.astype(BF16)
    return high, (value - high.astype(F32)).astype(BF16)


def dot3(a, b):
    def dot(p, q):
        return lax.dot_general(p, q, (((1,), (0,)), ((), ())), preferred_element_type=F32)

    return dot(a[0], b[0]) + (dot(a[0], b[1]) + dot(a[1], b[0]))


def lane_ids(shape):
    return lax.broadcasted_iota(jnp.int32, shape, len(shape) - 1)


def turn(value, shift):
    if isinstance(shift, int):
        shift = shift % LANES
        if shift == 0:
            return value
    else:
        shift = lax.rem(shift + 8 * LANES, LANES)
    return pltpu.roll(value, shift, axis=value.ndim - 1)


def pack_kernel(chunk, y_ref, x_ref, out_ref):
    y = y_ref[0]
    group = lane_ids((x_ref.shape[1], LANES)) // QUARTER
    for r in range(3):
        row = None
        for slot, plane in enumerate((r, r + 6, r + 3, r + 9)):
            piece = turn(x_ref[plane], QUARTER * slot - 64 - QUARTER * chunk + 64 * y)
            row = piece if row is None else jnp.where(group == slot, piece, row)
        out_ref[r] = row


def rim_pack(row, out_ref, r, source):
    part = row.shape[0] // 4
    group = lane_ids((part, LANES)) // QUARTER
    packed = None
    for j in range(4):
        piece = turn(row[j * part : (j + 1) * part], QUARTER * (j - source))
        packed = piece if packed is None else jnp.where(group == j, piece, packed)
    out_ref[pl.ds(r * part, part), :] = packed


def assemble_kernel(chunk, y_ref, x_ref, got_ref, v_ref, up_ref, down_ref):
    y = y_ref[0]
    group = lane_ids((x_ref.shape[1], LANES)) // QUARTER
    for r in range(6):
        first = turn(x_ref[r], -QUARTER * chunk)
        second = turn(x_ref[r + 6], QUARTER - QUARTER * chunk)
        other = turn(got_ref[r % 3], 64 * (1 - y) if r < 3 else 64 * y)
        row = jnp.where(group == 2 * y, first, jnp.where(group == 2 * y + 1, second, other))
        v_ref[r] = row
        rim_pack(row, up_ref, r, 3)
        rim_pack(row, down_ref, r, 0)


def collapse(blocks):
    group = lane_ids((32, LANES)) // QUARTER

    def block(i, s, target):
        b = 2 * i + s
        return turn(blocks[32 * b : 32 * b + 32], QUARTER * (target - i))

    low = block(0, 0, 0) + block(1, 0, 0) + block(2, 0, 0)
    high = block(1, 1, 1) + block(2, 1, 1) + block(3, 1, 1)
    below, above = block(0, 1, 2), block(3, 0, 3)
    return jnp.where(
        group == 0, low, jnp.where(group == 1, high, jnp.where(group == 2, below, above))
    )


def coef_kernel(v_ref, mh_ref, ml_ref, out_ref):
    total = None
    for r in range(6):
        term = dot3((mh_ref[r], ml_ref[r]), halves(v_ref[r]))
        total = term if total is None else total + term
    out_ref[...] = collapse(total)


def level_kernel(
    scale, recall, first, last, *refs
):
    refs = list(refs)
    v_ref = refs.pop(0)
    prev_ref = None if first else refs.pop(0)
    below_ref, above_ref = refs.pop(0), refs.pop(0)
    if first:
        below_coef, above_coef = refs.pop(0), refs.pop(0)
    own_ref, kb_ref, ch_ref, cl_ref, th_ref, tl_ref, pot_ref = refs[:7]
    refs = refs[7:]
    if last:
        y_ref, out_ref, send_ref, ext = refs
    else:
        mh_ref, ml_ref, out_ref, up_ref, down_ref, coef_ref, ext = refs
    cells = v_ref.shape[1]
    part = cells // 4
    rim = 6 * part
    group = lane_ids((cells, LANES)) // QUARTER
    part_group = lane_ids((part, LANES)) // QUARTER
    cg = lane_ids((32, LANES)) // QUARTER
    from_below = below_coef[...] if first else below_ref[pl.ds(rim, 32), :]
    from_above = above_coef[...] if first else above_ref[pl.ds(rim, 32), :]
    total = own_ref[...] + jnp.where(cg % 2 == 0, turn(from_below, 32), turn(from_above, -32))
    total = total * kb_ref[...]
    rows = []
    for i, s, source in (
        (0, 0, 0), (0, 1, 2), (1, 0, 0), (1, 1, 1), (2, 0, 0), (2, 1, 1), (3, 0, 3), (3, 1, 1),
    ):
        rows.append(jnp.where(cg == i, turn(total, QUARTER * (i - source)), 0.0))
    spread = halves(jnp.concatenate(rows, axis=0))
    for r in range(6):
        row = v_ref[r]
        ext[6 + r] = row
        before, after = turn(row, QUARTER), turn(row, -QUARTER)
        low, high = below_ref[pl.ds(r * part, part), :], above_ref[pl.ds(r * part, part), :]
        for j in range(4):
            cut = slice(j * part, (j + 1) * part)
            ext[r, cut] = jnp.where(part_group == 0, turn(low, -QUARTER * j), before[cut])
            ext[12 + r, cut] = jnp.where(part_group == 3, turn(high, 96 - QUARTER * j), after[cut])
    coef = None
    results = []
    for r in range(6):
        row = ext[6 + r]
        value = dot3((ch_ref[...], cl_ref[...]), halves(row))
        value = value + dot3((th_ref[r], tl_ref[r]), spread)
        value = value + pot_ref[r] * row
        for k in range(1, REACH + 1):
            value = value + (-0.5 * WEIGHTS[k]) * (ext[6 + r + k] + ext[6 + r - k])
        value = scale * value
        if not first:
            value = value - recall * prev_ref[r]
        out_ref[r] = value
        if last:
            results.append(value)
        else:
            rim_pack(value, up_ref, r, 3)
            rim_pack(value, down_ref, r, 0)
            term = dot3((mh_ref[r], ml_ref[r]), halves(value))
            coef = term if coef is None else coef + term
    if last:
        y = y_ref[0]
        for r in range(3):
            one = turn(out_ref[r], 64 * (1 - y))
            two = turn(out_ref[r + 3], 64 * y)
            send_ref[r] = jnp.where(group < 2, one, two)
    else:
        packed = collapse(coef)
        coef_ref[...] = packed
        up_ref[pl.ds(rim, 32), :] = packed
        down_ref[pl.ds(rim, 32), :] = packed


def unpack_kernel(yx_ref, v0_ref, v1_ref, r0_ref, r1_ref, out_ref, keep_ref, send_ref):
    y, x = yx_ref[0], yx_ref[1]
    group = lane_ids((v0_ref.shape[1], LANES)) // QUARTER
    for half in range(2):
        for r in range(6):
            row = None
            for k, (v_ref, r_ref) in enumerate(((v0_ref, r0_ref), (v1_ref, r1_ref))):
                own = turn(v_ref[r], QUARTER * (k - half))
                got = turn(
                    r_ref[r % 3],
                    64 * (1 - y) + QUARTER * (k - half) - (0 if r < 3 else 64),
                )
                mine = jnp.where(group == 2 * y + k, own, got)
                row = mine if k == 0 else jnp.where(group % 2 == k, mine, row)
            out_ref[6 * half + r] = row

    keep_ref[...] = out_ref[pl.ds(6 * x, 6)]
    send_ref[...] = out_ref[pl.ds(6 * (1 - x), 6)]


def gram_kernel(own_ref, xp_ref, sib_ref, sibxp_ref, keep_ref, send_ref):
    def dot(p, q):
        return lax.dot_general(p, q, (((0,), (0,)), ((), ())), preferred_element_type=F32)

    parts = [halves(ref[...]) for ref in (own_ref, xp_ref, sib_ref, sibxp_ref)]
    high = jnp.concatenate([p[0] for p in parts], axis=1)
    low = jnp.concatenate([p[1] for p in parts], axis=1)
    left_high, left_low = high[:, :256], low[:, :256]
    total = dot(left_high, high) + (dot(left_high, low) + dot(left_low, high))
    keep_ref[...] = total[:128]
    for j, source in enumerate((1, 0, 3, 2)):
        send_ref[:, j * 128 : (j + 1) * 128] = total[128:, source * 128 : (source + 1) * 128]


def order_kernel(factor, b_ref, keep_ref, got_ref, out_ref):
    b = b_ref[0]
    for j, flip in enumerate((0, 2, 1, 3)):
        cut = slice(j * 128, (j + 1) * 128)
        block = (keep_ref[:, cut] + got_ref[:, cut]) * factor
        target = pl.multiple_of(lax.bitwise_xor(b, flip) * 128, 128)
        out_ref[:, pl.ds(target, 128)] = block


def dense_kernel(yc_ref, planes_ref, proj_ref, e_ref, part_ref, rim_ref):
    y, c = yc_ref[0], yc_ref[1]
    e_ref[...] = jnp.zeros_like(e_ref)
    atoms, count, span, _ = proj_ref.shape
    for a in range(atoms):
        for b in range(span):
            plane = planes_ref[a, b]
            for p in range(count):
                at = (plane, pl.ds(a * count + p, 1), slice(None))
                e_ref[at] = e_ref[at] + proj_ref[a, p, pl.ds(b, 1), :]
    rows = pl.ds(pl.multiple_of(16 * c, 16), 16)
    part_ref[...] = e_ref[pl.ds(6 * (1 - y), 18), rows, :]
    rim_ref[...] = e_ref[pl.ds(18 * y, 6), rows, :]


def maps_kernel(
    yc_ref, e_ref, part_ref, part2_ref, a_ref, a2_ref, b_ref, b2_ref,
    mh_ref, ml_ref, th_ref, tl_ref,
):
    y, c = yc_ref[0], yc_ref[1]

    def whole(mine, other):
        first = jnp.where(c == 0, mine, other)
        second = jnp.where(c == 0, other, mine)
        return jnp.concatenate([first, second], axis=0)

    for r in range(6):
        one, two = whole(a_ref[r], a2_ref[r]), whole(b_ref[r], b2_ref[r])
        below, above = jnp.where(y == 1, one, two), jnp.where(y == 1, two, one)
        low = [
            jnp.where(
                y == 0, e_ref[6 + 6 * i + r], whole(part_ref[6 * i + r], part2_ref[6 * i + r])
            )
            for i in range(3)
        ]
        high = [
            jnp.where(y == 1, e_ref[6 * i + r], whole(part_ref[6 * i + r], part2_ref[6 * i + r]))
            for i in range(3)
        ]
        block = jnp.concatenate(
            [low[0], below, low[1], high[0], low[2], high[1], above, high[2]], axis=0
        )
        mh_ref[r], ml_ref[r] = halves(block)
        th_ref[r], tl_ref[r] = halves(block.T)


SMEM = pl.BlockSpec(memory_space=pltpu.SMEM)
VMEM = pl.BlockSpec(memory_space=pltpu.VMEM)


def call(kernel, out, scalars, arrays, scratch=(), flops=0):
    moved = sum(a.size * a.dtype.itemsize for a in arrays) + sum(
        int(np.prod(o.shape)) * o.dtype.itemsize for o in out
    )
    return pl.pallas_call(
        kernel,
        out_shape=out,
        in_specs=[SMEM] * len(scalars) + [VMEM] * len(arrays),
        out_specs=[VMEM] * len(out),
        scratch_shapes=list(scratch),
        compiler_params=pltpu.CompilerParams(vmem_limit_bytes=48 * 1024 * 1024),
        cost_estimate=pl.CostEstimate(flops=flops, bytes_accessed=moved, transcendentals=0),
    )(*scalars, *arrays)


def f32(*shape):
    return jax.ShapeDtypeStruct(shape, F32)


def bf16(*shape):
    return jax.ShapeDtypeStruct(shape, BF16)


def shards(orbitals, potential, projectors, atom_planes, kb_energy):
    slab, ny, nz, orb_here = orbitals.shape
    cells = ny * nz
    peers = lax.axis_size("grid")
    bands = lax.axis_size("band")
    g, b = lax.axis_index("grid"), lax.axis_index("band")
    y, c, x = lax.rem(g, 2), lax.rem(b, 2), b // 2
    y1 = y.reshape(1).astype(jnp.int32)
    b1 = b.reshape(1).astype(jnp.int32)
    yc = jnp.stack([y, c]).astype(jnp.int32)
    yx = jnp.stack([y, x]).astype(jnp.int32)

    def move(array, axis, target):
        size = lax.axis_size(axis)
        return lax.ppermute(array, axis, [(i, target(i) % size) for i in range(size)])

    def partner(array):
        return move(array, "grid", lambda i: i ^ 1)

    def up(array):
        return move(array, "grid", lambda i: i + 2)

    def down(array):
        return move(array, "grid", lambda i: i - 2)

    def sibling(array):
        return move(array, "band", lambda i: i ^ 1)

    def across(array):
        return move(array, "band", lambda i: i ^ 2)

    field = orbitals.reshape(slab, cells, orb_here)
    rim_rows = 6 * (cells // 4)
    middle, scales, recall = filter_terms(DEGREE)

    sent = [
        call(functools.partial(pack_kernel, k), [f32(3, cells, LANES)], [y1], [field])[0]
        for k in range(2)
    ]
    other = [partner(s) for s in sent]

    dense, part, rim = call(
        dense_kernel,
        [f32(24, 32, cells), f32(18, 16, cells), f32(6, 16, cells)],
        [yc, atom_planes],
        [projectors],
    )
    part = partner(part)
    rim_a = move(rim, "grid", lambda i: i + 2 if i % 2 else i - 2)
    rim_b = move(rim, "grid", lambda i: i + 1 if i % 2 else i - 1)
    mh, ml, th, tl = call(
        maps_kernel,
        [bf16(6, 256, cells)] * 2 + [bf16(6, cells, 256)] * 2,
        [yc],
        [dense, part, sibling(part), rim_a, sibling(rim_a), rim_b, sibling(rim_b)],
    )
    pot_other = partner(potential.reshape(slab, cells))
    pot_own = potential.reshape(slab, cells)
    pot = jnp.where(
        y == 0,
        jnp.concatenate([pot_own, pot_other]),
        jnp.concatenate([pot_other, pot_own]),
    )
    pot = pot - (middle + 0.5 * WEIGHTS[0])
    pot = jnp.repeat(pot.reshape(4, 6, cells).transpose(1, 2, 0), QUARTER, axis=-1)
    kb = jnp.broadcast_to(jnp.tile(kb_energy, 4)[:, None], (32, LANES))
    ch, cl = (jnp.asarray(m) for m in plane_matrix(ny, nz))

    chunks = []
    for k in range(2):
        v, rim_up, rim_down = call(
            functools.partial(assemble_kernel, k),
            [f32(6, cells, LANES), f32(rim_rows, LANES), f32(rim_rows, LANES)],
            [y1],
            [field, other[k]],
        )
        chunks.append(dict(v=v, prev=None, below=up(rim_up), above=down(rim_down)))
    for s in chunks:
        s["coef"] = call(coef_kernel, [f32(32, LANES)], [], [s["v"], mh, ml])[0]
        s["below_coef"], s["above_coef"] = up(s["coef"]), down(s["coef"])

    flops = 2 * 6 * 256 * 256 * 128
    for level in range(DEGREE):
        first, last = level == 0, level == DEGREE - 1
        for s in chunks:
            arrays = [s["v"]]
            if not first:
                arrays.append(s["prev"])
            arrays += [s["below"], s["above"]]
            if first:
                arrays += [s["below_coef"], s["above_coef"]]
            arrays += [s["coef"], kb, ch, cl, th, tl, pot]
            out = [f32(6, cells, LANES)]
            if last:
                out += [f32(3, cells, LANES)]
            else:
                arrays += [mh, ml]
                out += [f32(rim_rows + 32, LANES)] * 2 + [f32(32, LANES)]
            kernel = functools.partial(level_kernel, scales[level], recall[level], first, last)
            if last:
                order = len(arrays)
                made = pl.pallas_call(
                    kernel,
                    out_shape=out,
                    in_specs=[VMEM] * order + [SMEM],
                    out_specs=[VMEM] * 2,
                    scratch_shapes=[pltpu.VMEM((18, cells, LANES), F32)],
                    compiler_params=pltpu.CompilerParams(vmem_limit_bytes=48 * 1024 * 1024),
                    cost_estimate=pl.CostEstimate(
                        flops=6 * flops, bytes_accessed=8 << 20, transcendentals=0
                    ),
                )(*arrays, y1)
                s["prev"], s["v"] = s["v"], made[0]
                s["back"] = partner(made[1])
            else:
                made = call(
                    kernel, out, [], arrays, [pltpu.VMEM((18, cells, LANES), F32)], 9 * flops
                )
                s["prev"], s["v"], s["coef"] = s["v"], made[0], made[3]
                s["below"], s["above"] = up(made[1]), down(made[2])

    filtered, keep, send = call(
        unpack_kernel,
        [f32(slab, cells, LANES)] + [f32(6, cells, LANES)] * 2,
        [yx],
        [chunks[0]["v"], chunks[1]["v"], chunks[0]["back"], chunks[1]["back"]],
    )
    sib = sibling(keep)
    xp = across(send)
    sibxp = sibling(xp)
    flat = [a.reshape(6 * cells, LANES) for a in (keep, xp, sib, sibxp)]
    mine, theirs = call(
        gram_kernel, [f32(128, bands * 128)] * 2, [], flat, flops=6 * 6 * cells * 256 * 512
    )
    total = call(
        functools.partial(order_kernel, 1.0 / (slab * cells * peers)),
        [f32(128, bands * 128)],
        [b1],
        [mine, across(theirs)],
    )[0]
    pieces = total.reshape(peers, 128 // peers, bands * 128)
    pieces = lax.all_to_all(pieces, "grid", 0, 0)
    piece = jnp.broadcast_to(jnp.sum(pieces, axis=0, keepdims=True), pieces.shape)
    gram = lax.all_to_all(piece, "grid", 0, 0).reshape(128, bands * 128)
    return (filtered.reshape(orbitals.shape), gram)


def solution(mesh):
    return jax.shard_map(
        shards,
        mesh=mesh,
        in_specs=(
            P("grid", None, None, "band"),
            P("grid", None, None),
            P("grid", None, None, None),
            P("grid", None),
            P(),
        ),
        out_specs=(P("grid", None, None, "band"), P("band", None)),
        check_vma=False,
    )
```

```python
import functools

import jax
import jax.numpy as jnp
import ml_dtypes
import numpy as np
from jax import lax
from jax.experimental import pallas as pl
from jax.experimental.pallas import tpu as pltpu
from jax.sharding import PartitionSpec as P

DEGREE = 4
REACH = 6
LANES = 128
QUARTER = 32

WEIGHTS = (
    -5369.0 / 1800.0,
    12.0 / 7.0,
    -15.0 / 56.0,
    10.0 / 189.0,
    -1.0 / 112.0,
    2.0 / 1925.0,
    -1.0 / 16632.0,
)
LOWER = -4.0
CUTOFF = 1.0
UPPER = 16.0
F32 = jnp.float32
BF16 = jnp.bfloat16


def filter_terms(degree):
    half_span = (UPPER - CUTOFF) / 2.0
    middle = (UPPER + CUTOFF) / 2.0
    sigma_now = half_span / (LOWER - middle)
    sigma_first = sigma_now
    scales = [sigma_now / half_span]
    recall = [0.0]
    for level in range(1, degree):
        sigma_next = 1.0 / (2.0 / sigma_first - sigma_now)
        scales.append(2.0 * sigma_next / half_span)
        recall.append(sigma_now * sigma_next)
        sigma_now = sigma_next
    return (middle, scales, recall)


def plane_matrix(ny, nz):
    def ring(n):
        m = np.zeros((n, n))
        for i in range(n):
            m[i, i] += WEIGHTS[0]
            for r in range(1, REACH + 1):
                m[i, (i + r) % n] += WEIGHTS[r]
                m[i, (i - r) % n] += WEIGHTS[r]
        return m

    full = -0.5 * (np.kron(ring(ny), np.eye(nz)) + np.kron(np.eye(ny), ring(nz)))
    high = full.astype(ml_dtypes.bfloat16)
    low = (full - high.astype(np.float64)).astype(ml_dtypes.bfloat16)
    return high, low


def halves(value):
    high = value.astype(BF16)
    return high, (value - high.astype(F32)).astype(BF16)


def dot3(*pairs):
    left, right = [], []
    for (a_high, a_low), (b_high, b_low) in pairs:
        left += [a_high, a_high, a_low]
        right += [b_high, b_low, b_high]
    return lax.dot_general(
        jnp.concatenate(left, axis=1),
        jnp.concatenate(right, axis=0),
        (((1,), (0,)), ((), ())),
        preferred_element_type=F32,
    )


def lane_ids(shape):
    return lax.broadcasted_iota(jnp.int32, shape, len(shape) - 1)


def turn(value, shift):
    if isinstance(shift, int):
        shift = shift % LANES
        if shift == 0:
            return value
    else:
        shift = lax.rem(shift + 8 * LANES, LANES)
    return pltpu.roll(value, shift, axis=value.ndim - 1)


def pack_kernel(chunk, y_ref, x_ref, *refs):
    y = y_ref[0]
    out_ref = refs[-1]
    cells = x_ref.shape[1]
    group = lane_ids((cells, LANES)) // QUARTER
    if chunk:
        out_ref[3 * cells :] = refs[0][...]
    for r in range(3):
        row = None
        for slot, plane in enumerate((r, r + 6, r + 3, r + 9)):
            piece = turn(x_ref[plane], QUARTER * slot - 64 - QUARTER * chunk + 64 * y)
            row = piece if row is None else jnp.where(group == slot, piece, row)
        out_ref[r * cells : (r + 1) * cells] = row


def rim_pack(row, out_ref, r, source):
    part = row.shape[0] // 4
    group = lane_ids((part, LANES)) // QUARTER
    packed = None
    for j in range(4):
        piece = turn(row[j * part : (j + 1) * part], QUARTER * (j - source))
        packed = piece if packed is None else jnp.where(group == j, piece, packed)
    out_ref[pl.ds(r * part, part), :] = packed


def assemble_kernel(chunk, y_ref, x_ref, got_ref, *refs):
    y = y_ref[0]
    if chunk == 0:
        v_ref, up_ref, down_ref = refs
    else:
        mh_ref, ml_ref, v_ref, up_ref, down_ref, coef_ref = refs
    cells = x_ref.shape[1]
    group = lane_ids((cells, LANES)) // QUARTER
    coef = None
    for r in range(6):
        first = turn(x_ref[r], -QUARTER * chunk)
        second = turn(x_ref[r + 6], QUARTER - QUARTER * chunk)
        other = turn(
            got_ref[cells * (r % 3) : cells * (r % 3 + 1)], 64 * (1 - y) if r < 3 else 64 * y
        )
        row = jnp.where(group == 2 * y, first, jnp.where(group == 2 * y + 1, second, other))
        v_ref[r] = row
        rim_pack(row, up_ref, r, 3)
        rim_pack(row, down_ref, r, 0)
        if chunk:
            term = dot3(((mh_ref[r], ml_ref[r]), halves(row)))
            coef = term if coef is None else coef + term
    if chunk:
        share_coef(coef, coef_ref, up_ref, down_ref)


def share_coef(coef, coef_ref, up_ref, down_ref):
    packed = collapse(coef)
    coef_ref[...] = packed
    rim = up_ref.shape[0] - 32
    up_ref[pl.ds(rim, 32), :] = packed
    down_ref[pl.ds(rim, 32), :] = packed


def collapse(blocks):
    group = lane_ids((32, LANES)) // QUARTER

    def block(i, s, target):
        b = 2 * i + s
        return turn(blocks[32 * b : 32 * b + 32], QUARTER * (target - i))

    low = block(0, 0, 0) + block(1, 0, 0) + block(2, 0, 0)
    high = block(1, 1, 1) + block(2, 1, 1) + block(3, 1, 1)
    below, above = block(0, 1, 2), block(3, 0, 3)
    return jnp.where(
        group == 0, low, jnp.where(group == 1, high, jnp.where(group == 2, below, above))
    )


def coef_kernel(v_ref, mh_ref, ml_ref, out_ref):
    total = None
    for r in range(6):
        term = dot3(((mh_ref[r], ml_ref[r]), halves(v_ref[r])))
        total = term if total is None else total + term
    out_ref[...] = collapse(total)


def level_kernel(scale, recall, first, apart, last, joined, *refs):
    refs = list(refs)
    if last:
        yx_ref = refs.pop(0)
    v_ref = refs.pop(0)
    prev_ref = None if first else refs.pop(0)
    below_ref, above_ref = refs.pop(0), refs.pop(0)
    if apart:
        below_coef, above_coef = refs.pop(0), refs.pop(0)
    own_ref, kb_ref, ch_ref, cl_ref, th_ref, tl_ref, pot_ref = refs[:7]
    refs = refs[7:]
    if last:
        out_ref, own_piece, y_piece, x_piece, d_piece, ext = refs
    else:
        mh_ref, ml_ref, out_ref, up_ref, down_ref, coef_ref, ext = refs
    cells = v_ref.shape[1]
    part = cells // 4
    rim = 6 * part
    part_group = lane_ids((part, LANES)) // QUARTER
    cg = lane_ids((32, LANES)) // QUARTER
    from_below = below_coef[...] if apart else below_ref[pl.ds(rim, 32), :]
    from_above = above_coef[...] if apart else above_ref[pl.ds(rim, 32), :]
    total = own_ref[...] + jnp.where(cg % 2 == 0, turn(from_below, 32), turn(from_above, -32))
    total = total * kb_ref[...]
    rows = []
    for i, s, source in (
        (0, 0, 0), (0, 1, 2), (1, 0, 0), (1, 1, 1), (2, 0, 0), (2, 1, 1), (3, 0, 3), (3, 1, 1),
    ):
        rows.append(jnp.where(cg == i, turn(total, QUARTER * (i - source)), 0.0))
    spread = halves(jnp.concatenate(rows, axis=0))
    for r in range(6):
        row = v_ref[r]
        ext[6 + r] = row
        before, after = turn(row, QUARTER), turn(row, -QUARTER)
        low, high = below_ref[pl.ds(r * part, part), :], above_ref[pl.ds(r * part, part), :]
        for j in range(4):
            cut = slice(j * part, (j + 1) * part)
            ext[r, cut] = jnp.where(part_group == 0, turn(low, -QUARTER * j), before[cut])
            ext[12 + r, cut] = jnp.where(part_group == 3, turn(high, 96 - QUARTER * j), after[cut])
    coef = None
    if last:
        mine = 2 * yx_ref[0] + yx_ref[1]
    for r in range(6):
        row = ext[6 + r]
        value = dot3(
            ((ch_ref[...], cl_ref[...]), halves(row)), ((th_ref[r], tl_ref[r]), spread)
        )
        value = value + pot_ref[r] * row
        for k in range(1, REACH + 1):
            value = value + (-0.5 * WEIGHTS[k]) * (ext[6 + r + k] + ext[6 + r - k])
        value = scale * value
        if not first:
            value = value - recall * prev_ref[r]
        out_ref[r] = value
        if last:
            for flip, piece in enumerate((own_piece, x_piece, y_piece, d_piece)):
                rim_pack(value, piece, r, lax.bitwise_xor(mine, flip))
            if joined:
                y_piece[pl.ds(rim + r * part, part), :] = d_piece[pl.ds(r * part, part), :]
        else:
            rim_pack(value, up_ref, r, 3)
            rim_pack(value, down_ref, r, 0)
            term = dot3(((mh_ref[r], ml_ref[r]), halves(value)))
            coef = term if coef is None else coef + term
    if not last:
        share_coef(coef, coef_ref, up_ref, down_ref)


def unpack_kernel(yx_ref, v0_ref, v1_ref, y0_ref, y1_ref, rest_ref, out_ref):
    y, x = yx_ref[0], yx_ref[1]
    cells = v0_ref.shape[1]
    part = cells // 4
    group = lane_ids((part, LANES)) // QUARTER
    rim = 6 * part
    rest0_ref = y0_ref.at[pl.ds(rim, rim)]
    for half, pieces in ((x, (y0_ref, y1_ref)), (1 - x, (rest0_ref, rest_ref))):
        for r in range(6):
            own = [turn(v_ref[r], QUARTER * (k - half)) for k, v_ref in enumerate((v0_ref, v1_ref))]
            for j in range(4):
                rows = slice(j * part, (j + 1) * part)
                block = None
                for k in range(2):
                    got = turn(
                        pieces[k][pl.ds(r * part, part), :],
                        64 * (1 - y) + QUARTER * (k - j),
                    )
                    mine = jnp.where(group == 2 * y + k, own[k][rows], got)
                    block = mine if k == 0 else jnp.where(group % 2 == 1, mine, block)
                out_ref[6 * half + r, rows] = block


def tile_kernel(y_ref, own_ref, x_ref, y_piece_ref, d_ref, out_ref):
    y = y_ref[0]
    rows = own_ref.shape[0]
    pieces = [own_ref[...], y_piece_ref[pl.ds(0, rows)], x_ref[...], d_ref[...]]
    group = lane_ids((rows, LANES)) // QUARTER
    for j in range(4):
        block = None
        for s, piece in enumerate(pieces):
            target = 2 * (s // 2) + lax.bitwise_xor(y, s % 2)
            turned = turn(piece, QUARTER * (target - j))
            block = turned if block is None else jnp.where(group == target, turned, block)
        out_ref[pl.ds(j * rows, rows), :] = block


def gram_kernel(a0_ref, a1_ref, s0_ref, s1_ref, keep_ref, send_ref):
    def dot(p, q):
        return lax.dot_general(p, q, (((0,), (0,)), ((), ())), preferred_element_type=F32)

    parts = [halves(ref[...]) for ref in (a0_ref, a1_ref, s0_ref, s1_ref)]
    high = jnp.concatenate([p[0] for p in parts], axis=1)
    low = jnp.concatenate([p[1] for p in parts], axis=1)
    left_high, left_low = high[:, :256], low[:, :256]
    total = dot(left_high, high) + (dot(left_high, low) + dot(left_low, high))
    group = lane_ids((32, LANES)) // QUARTER
    for x_row, out_ref in ((0, keep_ref), (1, send_ref)):
        for h_row in range(2):
            for k_row in range(2):
                at = 128 * k_row + 64 * x_row + 32 * h_row
                for flip in range(4):
                    x_col, core = flip // 2, flip % 2
                    block = None
                    for h in range(2):
                        for k in range(2):
                            start = 256 * core + 128 * k
                            tile = total[at : at + 32, start : start + 128]
                            piece = turn(tile, QUARTER * (2 * h + k - 2 * x_col - h))
                            block = (
                                piece
                                if block is None
                                else jnp.where(group == 2 * h + k, piece, block)
                            )
                    to = 2 * (x_col ^ x_row) + core
                    out_ref[
                        pl.ds(64 * h_row + 32 * k_row, 32), 128 * to : 128 * to + 128
                    ] = block


def order_kernel(factor, b_ref, keep_ref, got_ref, out_ref):
    b = b_ref[0]
    for j, flip in enumerate((0, 1, 2, 3)):
        cut = slice(j * 128, (j + 1) * 128)
        block = (keep_ref[:, cut] + got_ref[:, cut]) * factor
        target = pl.multiple_of(lax.bitwise_xor(b, flip) * 128, 128)
        out_ref[:, pl.ds(target, 128)] = block


def dense_kernel(yc_ref, planes_ref, proj_ref, e_ref, part_ref, rim_ref):
    y, c = yc_ref[0], yc_ref[1]
    e_ref[...] = jnp.zeros_like(e_ref)
    atoms, span, count, _ = proj_ref.shape
    for a in range(atoms):
        for b in range(span):
            at = (planes_ref[a, b], slice(a * count, (a + 1) * count))
            e_ref[at] = e_ref[at] + proj_ref[a, b]
    rows = pl.ds(pl.multiple_of(16 * c, 16), 16)
    for r in range(18):
        part_ref[r] = e_ref[6 * (1 - y) + r, rows, :]
    rim_ref[...] = e_ref[pl.ds(18 * y, 6), rows, :]


def potential_kernel(offset, y_ref, own_ref, got_ref, out_ref):
    y = y_ref[0]
    cells = out_ref.shape[1]
    own = own_ref[...] + offset
    other = got_ref[3 * cells :] + offset
    first, second = jnp.where(y == 0, own, other), jnp.where(y == 0, other, own)
    whole = jnp.concatenate([first, second], axis=0)
    fill = jnp.zeros((LANES - whole.shape[0], LANES), F32)
    columns = jnp.concatenate([whole, fill], axis=0).T
    each = cells // LANES
    group = lane_ids((LANES, LANES)) // QUARTER
    for r in range(6):
        for h in range(each):
            row = None
            for i in range(4):
                at = (6 * i + r) * each + h
                piece = jnp.broadcast_to(columns[:, at : at + 1], (LANES, LANES))
                row = piece if row is None else jnp.where(group == i, piece, row)
            out_ref[r, h * LANES : (h + 1) * LANES] = row


def maps_kernel(
    yc_ref, e_ref, part_ref, part2_ref, a_ref, a2_ref, b_ref, b2_ref,
    mh_ref, ml_ref, th_ref, tl_ref,
):
    y, c = yc_ref[0], yc_ref[1]

    def whole(mine, rest):
        first, second = jnp.where(c == 0, mine, rest), jnp.where(c == 0, rest, mine)
        return jnp.concatenate([first, second], axis=0)

    for r in range(6):
        one, two = whole(a_ref[r], a2_ref[r]), whole(b_ref[r], b2_ref[r])
        below, above = jnp.where(y == 1, one, two), jnp.where(y == 1, two, one)
        other = [whole(part_ref[6 * i + r], part2_ref[6 * i + r]) for i in range(3)]
        low = [jnp.where(y == 0, e_ref[6 + 6 * i + r], other[i]) for i in range(3)]
        high = [jnp.where(y == 1, e_ref[6 * i + r], other[i]) for i in range(3)]
        block = jnp.concatenate(
            [low[0], below, low[1], high[0], low[2], high[1], above, high[2]], axis=0
        )
        mh_ref[r], ml_ref[r] = halves(block)
        th_ref[r], tl_ref[r] = halves(block.T)


SMEM = pl.BlockSpec(memory_space=pltpu.SMEM)
VMEM = pl.BlockSpec(memory_space=pltpu.VMEM)
ANY = pl.BlockSpec(memory_space=pl.ANY)


def call(kernel, out, scalars, arrays, scratch=(), after=()):
    used = len(scalars) + len(arrays)

    def body(*refs):
        kernel(*refs[:used], *refs[used + len(after) :])

    return pl.pallas_call(
        body,
        out_shape=out,
        in_specs=[SMEM] * len(scalars) + [VMEM] * len(arrays) + [ANY] * len(after),
        out_specs=[VMEM] * len(out),
        scratch_shapes=list(scratch),
        compiler_params=pltpu.CompilerParams(vmem_limit_bytes=48 * 1024 * 1024),
        cost_estimate=pl.CostEstimate(flops=1 << 10, bytes_accessed=1 << 10, transcendentals=0),
    )(*scalars, *arrays, *after)


def f32(*shape):
    return jax.ShapeDtypeStruct(shape, F32)


def bf16(*shape):
    return jax.ShapeDtypeStruct(shape, BF16)


def shards(orbitals, potential, projectors, atom_planes, kb_energy):
    slab, ny, nz, orb_here = orbitals.shape
    cells = ny * nz
    peers = lax.axis_size("grid")
    bands = lax.axis_size("band")
    g, b = lax.axis_index("grid"), lax.axis_index("band")
    y, c, x = lax.rem(g, 2), lax.rem(b, 2), b // 2
    y1 = y.reshape(1).astype(jnp.int32)
    b1 = b.reshape(1).astype(jnp.int32)
    yc = jnp.stack([y, c]).astype(jnp.int32)
    yx = jnp.stack([y, x]).astype(jnp.int32)

    def move(array, axis, target):
        size = lax.axis_size(axis)
        return lax.ppermute(array, axis, [(i, target(i) % size) for i in range(size)])

    def partner(array):
        return move(array, "grid", lambda i: i ^ 1)

    def up(array):
        return move(array, "grid", lambda i: i + 2)

    def down(array):
        return move(array, "grid", lambda i: i - 2)

    def sibling(array):
        return move(array, "band", lambda i: i ^ 1)

    def across(array):
        return move(array, "band", lambda i: i ^ 2)

    field = orbitals.reshape(slab, cells, orb_here)
    rim_rows = 6 * (cells // 4)
    middle, scales, recall = filter_terms(DEGREE)

    def diagonal(array):
        size = peers * bands
        flip = 2 * peers + 1
        return lax.ppermute(array, ("band", "grid"), [(i, i ^ flip) for i in range(size)])

    pot_own = potential.reshape(slab * cells // LANES, LANES)
    pot_rows = pot_own.shape[0]
    sent0 = call(
        functools.partial(pack_kernel, 0), [f32(3 * cells, LANES)], [y1], [field]
    )[0]
    other0 = partner(sent0)
    dense, part, rim = call(
        dense_kernel,
        [f32(24, 32, cells), f32(18, 16, cells), f32(6, 16, cells)],
        [yc, atom_planes],
        [projectors.transpose(0, 2, 1, 3)],
        after=[sent0],
    )
    part = partner(part)
    rim_a = move(rim, "grid", lambda i: i + 2 if i % 2 else i - 2)
    rim_b = move(rim, "grid", lambda i: i + 1 if i % 2 else i - 1)
    sent1 = call(
        functools.partial(pack_kernel, 1),
        [f32(3 * cells + pot_rows, LANES)],
        [y1],
        [field, pot_own],
        after=[other0],
    )[0]
    other1 = partner(sent1)
    other = [other0, other1]
    first_made = call(
        functools.partial(assemble_kernel, 0),
        [f32(6, cells, LANES)] + [f32(rim_rows, LANES)] * 2,
        [y1],
        [field, other0],
    )
    part, rim_a, rim_b, v0 = lax.optimization_barrier((part, rim_a, rim_b, first_made[0]))
    mh, ml, th, tl = call(
        maps_kernel,
        [bf16(6, 256, cells)] * 2 + [bf16(6, cells, 256)] * 2,
        [yc],
        [dense, part, sibling(part), rim_a, sibling(rim_a), rim_b, sibling(rim_b)],
    )
    pot = call(
        functools.partial(potential_kernel, -(middle + 0.5 * WEIGHTS[0])),
        [f32(6, cells, LANES)],
        [y1],
        [pot_own, other1],
    )[0]
    kb = jnp.broadcast_to(jnp.tile(kb_energy, 4)[:, None], (32, LANES))
    ch, cl = (jnp.asarray(m) for m in plane_matrix(ny, nz))

    s = dict(v=v0, prev=None, below=up(first_made[1]), above=down(first_made[2]))
    s["coef"] = call(coef_kernel, [f32(32, LANES)], [], [v0, mh, ml])[0]
    s["apart"] = [up(s["coef"]), down(s["coef"])]
    made = call(
        functools.partial(assemble_kernel, 1),
        [f32(6, cells, LANES)] + [f32(rim_rows + 32, LANES)] * 2 + [f32(32, LANES)],
        [y1],
        [field, other1, mh, ml],
        after=[s["coef"]],
    )
    up1, down1, s["apart"] = lax.optimization_barrier((made[1], made[2], s["apart"]))
    chunks = [
        s,
        dict(v=made[0], prev=None, below=up(up1), above=down(down1), coef=made[3]),
    ]

    for level in range(DEGREE):
        first, last = level == 0, level == DEGREE - 1
        for k, s in enumerate(chunks):
            apart = s.pop("apart", [])
            arrays = [s["v"]] + ([] if first else [s["prev"]]) + [s["below"], s["above"]]
            arrays += apart + [s["coef"], kb, ch, cl, th, tl, pot]
            out = [f32(6, cells, LANES)]
            if last:
                out += [f32(rim_rows * n, LANES) for n in (1, 2 - k, 1, 1)]
            else:
                arrays += [mh, ml]
                out += [f32(rim_rows + 32, LANES)] * 2 + [f32(32, LANES)]
            made = call(
                functools.partial(
                    level_kernel, scales[level], recall[level], first, bool(apart), last, k == 0
                ),
                out,
                [yx] if last else [],
                arrays,
                [pltpu.VMEM((18, cells, LANES), F32)],
            )
            s["prev"], s["v"] = s["v"], made[0]
            if last:
                s["pieces"] = [made[1], across(made[3]), partner(made[2]), diagonal(made[4])]
                rest = made[4]
            else:
                s["coef"], s["below"], s["above"] = made[3], up(made[1]), down(made[2])

    tiles = [
        call(tile_kernel, [f32(4 * rim_rows, LANES)], [y1], s["pieces"])[0] for s in chunks
    ]
    mine, theirs = call(
        gram_kernel,
        [f32(128, bands * 128)] * 2,
        [],
        tiles + [sibling(t) for t in tiles],
    )
    rest = partner(rest)
    filtered = call(
        unpack_kernel,
        [f32(slab, cells, LANES)],
        [yx],
        [s["v"] for s in chunks] + [s["pieces"][2] for s in chunks] + [rest],
    )[0]
    total = call(
        functools.partial(order_kernel, 1.0 / (slab * cells * peers)),
        [f32(128, bands * 128)],
        [b1],
        [mine, across(theirs)],
        after=[rest],
    )[0]
    pieces = total.reshape(peers, 128 // peers, bands * 128)
    pieces = lax.all_to_all(pieces, "grid", 0, 0)
    piece = jnp.broadcast_to(jnp.sum(pieces, axis=0, keepdims=True), pieces.shape)
    gram = lax.all_to_all(piece, "grid", 0, 0).reshape(128, bands * 128)
    return (filtered.reshape(orbitals.shape), gram)


def solution(mesh):
    return jax.shard_map(
        shards,
        mesh=mesh,
        in_specs=(
            P("grid", None, None, "band"),
            P("grid", None, None),
            P("grid", None, None, None),
            P("grid", None),
            P(),
        ),
        out_specs=(P("grid", None, None, "band"), P("band", None)),
        check_vma=False,
    )
```

```python
import functools

import jax
import jax.numpy as jnp
import ml_dtypes
import numpy as np
from jax import lax
from jax.experimental import pallas as pl
from jax.experimental.pallas import tpu as pltpu
from jax.sharding import PartitionSpec as P

DEGREE = 4
REACH = 6
LANES = 128
QUARTER = 32

WEIGHTS = (
    -5369.0 / 1800.0,
    12.0 / 7.0,
    -15.0 / 56.0,
    10.0 / 189.0,
    -1.0 / 112.0,
    2.0 / 1925.0,
    -1.0 / 16632.0,
)
LOWER = -4.0
CUTOFF = 1.0
UPPER = 16.0
F32 = jnp.float32
BF16 = jnp.bfloat16


def filter_terms(degree):
    half_span = (UPPER - CUTOFF) / 2.0
    middle = (UPPER + CUTOFF) / 2.0
    sigma_now = half_span / (LOWER - middle)
    sigma_first = sigma_now
    scales = [sigma_now / half_span]
    recall = [0.0]
    for level in range(1, degree):
        sigma_next = 1.0 / (2.0 / sigma_first - sigma_now)
        scales.append(2.0 * sigma_next / half_span)
        recall.append(sigma_now * sigma_next)
        sigma_now = sigma_next
    return (middle, scales, recall)


def plane_matrix(ny, nz):
    def ring(n):
        m = np.zeros((n, n))
        for i in range(n):
            m[i, i] += WEIGHTS[0]
            for r in range(1, REACH + 1):
                m[i, (i + r) % n] += WEIGHTS[r]
                m[i, (i - r) % n] += WEIGHTS[r]
        return m

    full = -0.5 * (np.kron(ring(ny), np.eye(nz)) + np.kron(np.eye(ny), ring(nz)))
    high = full.astype(ml_dtypes.bfloat16)
    low = (full - high.astype(np.float64)).astype(ml_dtypes.bfloat16)
    return high, low


def halves(value):
    high = value.astype(BF16)
    return high, (value - high.astype(F32)).astype(BF16)


def dot3(*pairs):
    left, right = [], []
    for (a_high, a_low), (b_high, b_low) in pairs:
        left += [a_high, a_high, a_low]
        right += [b_high, b_low, b_high]
    return lax.dot_general(
        jnp.concatenate(left, axis=1),
        jnp.concatenate(right, axis=0),
        (((1,), (0,)), ((), ())),
        preferred_element_type=F32,
    )


def lane_ids(shape):
    return lax.broadcasted_iota(jnp.int32, shape, len(shape) - 1)


def turn(value, shift):
    if isinstance(shift, int):
        shift = shift % LANES
        if shift == 0:
            return value
    else:
        shift = lax.rem(shift + 8 * LANES, LANES)
    return pltpu.roll(value, shift, axis=value.ndim - 1)


def pack_kernel(chunk, y_ref, x_ref, *refs):
    y = y_ref[0]
    out_ref = refs[-1]
    cells = x_ref.shape[1]
    group = lane_ids((cells, LANES)) // QUARTER
    if len(refs) > 1:
        out_ref[3 * cells :] = refs[0][...]
    for r in range(3):
        row = None
        for slot, plane in enumerate((r, r + 6, r + 3, r + 9)):
            piece = turn(x_ref[plane], QUARTER * slot - 64 - QUARTER * chunk + 64 * y)
            row = piece if row is None else jnp.where(group == slot, piece, row)
        out_ref[r * cells : (r + 1) * cells] = row


def rim_pack(row, out_ref, r, source):
    part = row.shape[0] // 4
    group = lane_ids((part, LANES)) // QUARTER
    packed = None
    for j in range(4):
        piece = turn(row[j * part : (j + 1) * part], QUARTER * (j - source))
        packed = piece if packed is None else jnp.where(group == j, piece, packed)
    out_ref[pl.ds(r * part, part), :] = packed


def assemble_kernel(chunk, y_ref, x_ref, got_ref, *refs):
    y = y_ref[0]
    mh_ref, ml_ref, v_ref, up_ref, down_ref, coef_ref = refs
    cells = x_ref.shape[1]
    group = lane_ids((cells, LANES)) // QUARTER
    coef = None
    for r in range(6):
        first = turn(x_ref[r], -QUARTER * chunk)
        second = turn(x_ref[r + 6], QUARTER - QUARTER * chunk)
        other = turn(
            got_ref[cells * (r % 3) : cells * (r % 3 + 1)], 64 * (1 - y) if r < 3 else 64 * y
        )
        row = jnp.where(group == 2 * y, first, jnp.where(group == 2 * y + 1, second, other))
        v_ref[r] = row
        rim_pack(row, up_ref, r, 3)
        rim_pack(row, down_ref, r, 0)
        term = dot3(((mh_ref[r], ml_ref[r]), halves(row)))
        coef = term if coef is None else coef + term
    share_coef(coef, coef_ref, up_ref, down_ref)


def share_coef(coef, coef_ref, up_ref, down_ref):
    packed = collapse(coef)
    coef_ref[...] = packed
    rim = up_ref.shape[0] - 32
    up_ref[pl.ds(rim, 32), :] = packed
    down_ref[pl.ds(rim, 32), :] = packed


def collapse(blocks):
    group = lane_ids((32, LANES)) // QUARTER

    def block(i, s, target):
        b = 2 * i + s
        return turn(blocks[32 * b : 32 * b + 32], QUARTER * (target - i))

    low = block(0, 0, 0) + block(1, 0, 0) + block(2, 0, 0)
    high = block(1, 1, 1) + block(2, 1, 1) + block(3, 1, 1)
    below, above = block(0, 1, 2), block(3, 0, 3)
    return jnp.where(
        group == 0, low, jnp.where(group == 1, high, jnp.where(group == 2, below, above))
    )


def level_kernel(scale, recall, first, last, *refs):
    refs = list(refs)
    if last:
        yx_ref = refs.pop(0)
    v_ref = refs.pop(0)
    prev_ref = None if first else refs.pop(0)
    below_ref, above_ref = refs.pop(0), refs.pop(0)
    own_ref, kb_ref, ch_ref, cl_ref, th_ref, tl_ref, pot_ref = refs[:7]
    refs = refs[7:]
    if last:
        out_ref, own_piece, y_piece, x_piece, d_piece, ext = refs
    else:
        mh_ref, ml_ref, out_ref, up_ref, down_ref, coef_ref, ext = refs
    cells = v_ref.shape[1]
    part = cells // 4
    rim = 6 * part
    part_group = lane_ids((part, LANES)) // QUARTER
    cg = lane_ids((32, LANES)) // QUARTER
    from_below = below_ref[pl.ds(rim, 32), :]
    from_above = above_ref[pl.ds(rim, 32), :]
    total = own_ref[...] + jnp.where(cg % 2 == 0, turn(from_below, 32), turn(from_above, -32))
    total = total * kb_ref[...]
    rows = []
    for i, s, source in (
        (0, 0, 0), (0, 1, 2), (1, 0, 0), (1, 1, 1), (2, 0, 0), (2, 1, 1), (3, 0, 3), (3, 1, 1),
    ):
        rows.append(jnp.where(cg == i, turn(total, QUARTER * (i - source)), 0.0))
    spread = halves(jnp.concatenate(rows, axis=0))
    for r in range(6):
        row = v_ref[r]
        ext[6 + r] = row
        before, after = turn(row, QUARTER), turn(row, -QUARTER)
        low, high = below_ref[pl.ds(r * part, part), :], above_ref[pl.ds(r * part, part), :]
        for j in range(4):
            cut = slice(j * part, (j + 1) * part)
            ext[r, cut] = jnp.where(part_group == 0, turn(low, -QUARTER * j), before[cut])
            ext[12 + r, cut] = jnp.where(part_group == 3, turn(high, 96 - QUARTER * j), after[cut])
    coef = None
    if last:
        mine = 2 * yx_ref[0] + yx_ref[1]
    for r in range(6):
        row = ext[6 + r]
        value = dot3(
            ((ch_ref[...], cl_ref[...]), halves(row)), ((th_ref[r], tl_ref[r]), spread)
        )
        value = value + pot_ref[r] * row
        for k in range(1, REACH + 1):
            value = value + (-0.5 * WEIGHTS[k]) * (ext[6 + r + k] + ext[6 + r - k])
        value = scale * value
        if not first:
            value = value - recall * prev_ref[r]
        out_ref[r] = value
        if last:
            for flip, piece in enumerate((own_piece, x_piece, y_piece, d_piece)):
                rim_pack(value, piece, r, lax.bitwise_xor(mine, flip))
        else:
            rim_pack(value, up_ref, r, 3)
            rim_pack(value, down_ref, r, 0)
            term = dot3(((mh_ref[r], ml_ref[r]), halves(value)))
            coef = term if coef is None else coef + term
    if not last:
        share_coef(coef, coef_ref, up_ref, down_ref)


def unpack_kernel(yx_ref, v0_ref, v1_ref, y0_ref, y1_ref, o0_ref, o1_ref, out_ref):
    y, x = yx_ref[0], yx_ref[1]
    cells = v0_ref.shape[1]
    part = cells // 4
    group = lane_ids((part, LANES)) // QUARTER
    for half, pieces in ((x, (y0_ref, y1_ref)), (1 - x, (o0_ref, o1_ref))):
        for r in range(6):
            own = [turn(v_ref[r], QUARTER * (k - half)) for k, v_ref in enumerate((v0_ref, v1_ref))]
            for j in range(4):
                rows = slice(j * part, (j + 1) * part)
                block = None
                for k in range(2):
                    got = turn(
                        pieces[k][pl.ds(r * part, part), :],
                        64 * (1 - y) + QUARTER * (k - j),
                    )
                    mine = jnp.where(group == 2 * y + k, own[k][rows], got)
                    block = mine if k == 0 else jnp.where(group % 2 == 1, mine, block)
                out_ref[6 * half + r, rows] = block


def tile_kernel(y_ref, own_ref, x_ref, y_piece_ref, d_ref, out_ref):
    y = y_ref[0]
    rows = own_ref.shape[0]
    pieces = [own_ref[...], y_piece_ref[...], x_ref[...], d_ref[...]]
    group = lane_ids((rows, LANES)) // QUARTER
    for j in range(4):
        block = None
        for s, piece in enumerate(pieces):
            target = 2 * (s // 2) + lax.bitwise_xor(y, s % 2)
            turned = turn(piece, QUARTER * (target - j))
            block = turned if block is None else jnp.where(group == target, turned, block)
        out_ref[pl.ds(j * rows, rows), :] = block


def gram_kernel(
    y_ref, a0_ref, a1_ref, s0_ref, s1_ref, own_ref, to_y_ref, to_x_ref, to_d_ref, parts_ref
):
    def dot(p, q):
        return lax.dot_general(p, q, (((0,), (0,)), ((), ())), preferred_element_type=F32)

    parts = [halves(ref[...]) for ref in (a0_ref, a1_ref, s0_ref, s1_ref)]
    high = jnp.concatenate([p[0] for p in parts], axis=1)
    low = jnp.concatenate([p[1] for p in parts], axis=1)
    left_high, left_low = high[:, :256], low[:, :256]
    total = dot(left_high, high) + (dot(left_high, low) + dot(left_low, high))
    group = lane_ids((32, LANES)) // QUARTER
    for x_row in range(2):
        for h_row in range(2):
            for k_row in range(2):
                at = 128 * k_row + 64 * x_row + 32 * h_row
                for flip in range(4):
                    x_col, core = flip // 2, flip % 2
                    block = None
                    for h in range(2):
                        for k in range(2):
                            start = 256 * core + 128 * k
                            tile = total[at : at + 32, start : start + 128]
                            piece = turn(tile, QUARTER * (2 * h + k - 2 * x_col - h))
                            block = (
                                piece
                                if block is None
                                else jnp.where(group == 2 * h + k, piece, block)
                            )
                    to = 2 * (x_col ^ x_row) + core
                    rows = slice(32 * k_row, 32 * k_row + 32)
                    parts_ref[2 * x_row + h_row, rows, 128 * to : 128 * to + 128] = block
    y = y_ref[0]
    own_ref[...] = parts_ref[y]
    to_y_ref[...] = parts_ref[1 - y]
    to_x_ref[...] = parts_ref[2 + y]
    to_d_ref[...] = parts_ref[3 - y]


def add_kernel(*refs):
    *terms, out_ref = refs
    out_ref[...] = (terms[0][...] + terms[1][...]) + (terms[2][...] + terms[3][...])


def ring_add_kernel(factor, z_ref, *refs):
    *terms, out_ref, slots = refs
    count = len(terms)
    for k, term in enumerate(terms):
        slots[lax.rem(z_ref[0] - k + count, count)] = term[...]
    total = slots[0]
    for k in range(1, count):
        total = total + slots[k]
    out_ref[...] = total * factor


def scale_kernel(factor, in_ref, out_ref):
    out_ref[...] = in_ref[...] * factor


def order_kernel(yb_ref, mine_ref, got_ref, out_ref):
    y, b = yb_ref[0], yb_ref[1]
    half = mine_ref.shape[0]
    for ref, h in ((mine_ref, y), (got_ref, 1 - y)):
        rows = pl.ds(pl.multiple_of(half * h, half), half)
        for j in range(4):
            to = pl.multiple_of(lax.bitwise_xor(b, j) * 128, 128)
            out_ref[rows, pl.ds(to, 128)] = ref[:, j * 128 : (j + 1) * 128]


def dense_kernel(yc_ref, planes_ref, proj_ref, e_ref, part_ref, rim_ref):
    y, c = yc_ref[0], yc_ref[1]
    e_ref[...] = jnp.zeros_like(e_ref)
    atoms, span, count, _ = proj_ref.shape
    for a in range(atoms):
        for b in range(span):
            at = (planes_ref[a, b], slice(a * count, (a + 1) * count))
            e_ref[at] = e_ref[at] + proj_ref[a, b]
    rows = pl.ds(pl.multiple_of(16 * c, 16), 16)
    for r in range(18):
        part_ref[r] = e_ref[6 * (1 - y) + r, rows, :]
    rim_ref[...] = e_ref[pl.ds(18 * y, 6), rows, :]


def potential_kernel(offset, y_ref, own_ref, got_ref, out_ref):
    y = y_ref[0]
    cells = out_ref.shape[1]
    own = own_ref[...] + offset
    other = got_ref[3 * cells :] + offset
    first, second = jnp.where(y == 0, own, other), jnp.where(y == 0, other, own)
    whole = jnp.concatenate([first, second], axis=0)
    fill = jnp.zeros((LANES - whole.shape[0], LANES), F32)
    columns = jnp.concatenate([whole, fill], axis=0).T
    each = cells // LANES
    group = lane_ids((LANES, LANES)) // QUARTER
    for r in range(6):
        for h in range(each):
            row = None
            for i in range(4):
                at = (6 * i + r) * each + h
                piece = jnp.broadcast_to(columns[:, at : at + 1], (LANES, LANES))
                row = piece if row is None else jnp.where(group == i, piece, row)
            out_ref[r, h * LANES : (h + 1) * LANES] = row


def gather_kernel(y_ref, part_ref, a_ref, b_ref, out_ref):
    y = y_ref[0]
    out_ref[:18] = part_ref[...]
    for r in range(6):
        one, two = a_ref[r], b_ref[r]
        out_ref[18 + r] = jnp.where(y == 1, one, two)
        out_ref[24 + r] = jnp.where(y == 1, two, one)


def maps_kernel(yc_ref, e_ref, part_ref, part2_ref, mh_ref, ml_ref, th_ref, tl_ref):
    y, c = yc_ref[0], yc_ref[1]

    def whole(plane):
        mine, rest = part_ref[plane], part2_ref[plane]
        first, second = jnp.where(c == 0, mine, rest), jnp.where(c == 0, rest, mine)
        return jnp.concatenate([first, second], axis=0)

    for r in range(6):
        below, above = whole(18 + r), whole(24 + r)
        other = [whole(6 * i + r) for i in range(3)]
        low = [jnp.where(y == 0, e_ref[6 + 6 * i + r], other[i]) for i in range(3)]
        high = [jnp.where(y == 1, e_ref[6 * i + r], other[i]) for i in range(3)]
        block = jnp.concatenate(
            [low[0], below, low[1], high[0], low[2], high[1], above, high[2]], axis=0
        )
        mh_ref[r], ml_ref[r] = halves(block)
        th_ref[r], tl_ref[r] = halves(block.T)


SMEM = pl.BlockSpec(memory_space=pltpu.SMEM)
VMEM = pl.BlockSpec(memory_space=pltpu.VMEM)
ANY = pl.BlockSpec(memory_space=pl.ANY)


def call(kernel, out, scalars, arrays, scratch=(), after=()):
    used = len(scalars) + len(arrays)

    def body(*refs):
        kernel(*refs[:used], *refs[used + len(after) :])

    return pl.pallas_call(
        body,
        out_shape=out,
        in_specs=[SMEM] * len(scalars) + [VMEM] * len(arrays) + [ANY] * len(after),
        out_specs=[VMEM] * len(out),
        scratch_shapes=list(scratch),
        compiler_params=pltpu.CompilerParams(vmem_limit_bytes=16 * 1024 * 1024),
        cost_estimate=pl.CostEstimate(flops=1 << 10, bytes_accessed=1 << 10, transcendentals=0),
    )(*scalars, *arrays, *after)


def f32(*shape):
    return pltpu.VMEM(shape, F32)


def bf16(*shape):
    return pltpu.VMEM(shape, BF16)


def shards(orbitals, potential, projectors, atom_planes, kb_energy):
    slab, ny, nz, orb_here = orbitals.shape
    cells = ny * nz
    peers = lax.axis_size("grid")
    bands = lax.axis_size("band")
    g, b = lax.axis_index("grid"), lax.axis_index("band")
    y, c, x = lax.rem(g, 2), lax.rem(b, 2), b // 2
    y1 = y.reshape(1).astype(jnp.int32)
    z1 = (g // 2).reshape(1).astype(jnp.int32)
    yb = jnp.stack([y, b]).astype(jnp.int32)
    yc = jnp.stack([y, c]).astype(jnp.int32)
    yx = jnp.stack([y, x]).astype(jnp.int32)

    def move(array, axis, target):
        size = lax.axis_size(axis)
        return lax.ppermute(array, axis, [(i, target(i) % size) for i in range(size)])

    def partner(array):
        return move(array, "grid", lambda i: i ^ 1)

    def up(array):
        return move(array, "grid", lambda i: i + 2)

    def down(array):
        return move(array, "grid", lambda i: i - 2)

    def sibling(array):
        return move(array, "band", lambda i: i ^ 1)

    def across(array):
        return move(array, "band", lambda i: i ^ 2)

    field = orbitals.reshape(slab, cells, orb_here)
    rim_rows = 6 * (cells // 4)
    middle, scales, recall = filter_terms(DEGREE)

    def diagonal(array):
        size = peers * bands
        flip = 2 * peers + 1
        return lax.ppermute(array, ("band", "grid"), [(i, i ^ flip) for i in range(size)])

    pot_own = potential.reshape(slab * cells // LANES, LANES)
    pot_rows = pot_own.shape[0]
    sent0 = call(
        functools.partial(pack_kernel, 0), [f32(3 * cells, LANES)], [y1], [field]
    )[0]
    other0 = partner(sent0)
    dense, part, rim = call(
        dense_kernel,
        [f32(24, 32, cells), f32(18, 16, cells), f32(6, 16, cells)],
        [yc, atom_planes],
        [projectors.transpose(0, 2, 1, 3)],
        after=[sent0],
    )
    part = partner(part)
    rim_a = move(rim, "grid", lambda i: i + 2 if i % 2 else i - 2)
    rim_b = move(rim, "grid", lambda i: i + 1 if i % 2 else i - 1)
    sent1 = call(
        functools.partial(pack_kernel, 1),
        [f32(3 * cells + pot_rows, LANES)],
        [y1],
        [field, pot_own],
        after=[other0],
    )[0]
    other1 = partner(sent1)
    part = call(
        gather_kernel, [f32(30, 16, cells)], [y1], [part, rim_a, rim_b], after=[sent1]
    )[0]
    mh, ml, th, tl = call(
        maps_kernel,
        [bf16(6, 256, cells)] * 2 + [bf16(6, cells, 256)] * 2,
        [yc],
        [dense, part, sibling(part)],
    )
    pot = call(
        functools.partial(potential_kernel, -(middle + 0.5 * WEIGHTS[0])),
        [f32(6, cells, LANES)],
        [y1],
        [pot_own, other1],
    )[0]
    kb = jnp.broadcast_to(jnp.tile(kb_energy, 4)[:, None], (32, LANES))
    ch, cl = (jnp.asarray(m) for m in plane_matrix(ny, nz))

    chunks = []
    for k, got in enumerate((other0, other1)):
        made = call(
            functools.partial(assemble_kernel, k),
            [f32(6, cells, LANES)] + [f32(rim_rows + 32, LANES)] * 2 + [f32(32, LANES)],
            [y1],
            [field, got, mh, ml],
        )
        chunks.append(
            dict(v=made[0], prev=None, below=up(made[1]), above=down(made[2]), coef=made[3])
        )

    for level in range(DEGREE):
        first, last = level == 0, level == DEGREE - 1
        for s in chunks:
            arrays = [s["v"]] + ([] if first else [s["prev"]]) + [s["below"], s["above"]]
            arrays += [s["coef"], kb, ch, cl, th, tl, pot]
            out = [f32(6, cells, LANES)]
            if last:
                out += [f32(rim_rows, LANES)] * 4
            else:
                arrays += [mh, ml]
                out += [f32(rim_rows + 32, LANES)] * 2 + [f32(32, LANES)]
            made = call(
                functools.partial(level_kernel, scales[level], recall[level], first, last),
                out,
                [yx] if last else [],
                arrays,
                [pltpu.VMEM((18, cells, LANES), F32)],
            )
            s["prev"], s["v"] = s["v"], made[0]
            if last:
                s["pieces"] = [made[1], across(made[3]), partner(made[2]), diagonal(made[4])]
                s["rest"] = made[4]
            else:
                s["coef"], s["below"], s["above"] = made[3], up(made[1]), down(made[2])

    tiles = [
        call(tile_kernel, [f32(4 * rim_rows, LANES)], [y1], s["pieces"])[0] for s in chunks
    ]
    quarters = call(
        gram_kernel,
        [f32(64, bands * 128)] * 4,
        [y1],
        tiles + [sibling(t) for t in tiles],
        [pltpu.VMEM((4, 64, bands * 128), F32)],
    )
    partial = call(
        add_kernel,
        [f32(64, bands * 128)],
        [],
        [quarters[0], partner(quarters[1]), across(quarters[2]), diagonal(quarters[3])],
    )[0]
    rest0, rest1, partial = lax.optimization_barrier(
        (chunks[0]["rest"], chunks[1]["rest"], partial)
    )
    rest = [partner(rest0), partner(rest1)]
    factor = 1.0 / (slab * cells * peers)
    pairs = peers // 2
    if pairs <= 4:
        moved = [partial]
        for k in range(1, pairs):
            moved.append(move(partial, "grid", lambda i, k=k: i + 2 * k))
        total = call(
            functools.partial(ring_add_kernel, factor),
            [f32(64, bands * 128)],
            [z1],
            moved,
            [pltpu.VMEM((pairs, 64, bands * 128), F32)],
            after=rest,
        )[0]
    else:
        groups = [[2 * i + j for i in range(pairs)] for j in range(2)]
        total = lax.psum(partial, "grid", axis_index_groups=groups)
        total = call(
            functools.partial(scale_kernel, factor), [f32(64, bands * 128)], [], [total]
        )[0]
    gram = call(
        order_kernel,
        [jax.ShapeDtypeStruct((128, bands * 128), F32)],
        [yb],
        [total, partner(total)],
    )[0]
    filtered = call(
        unpack_kernel,
        [jax.ShapeDtypeStruct((slab, cells, LANES), F32)],
        [yx],
        [s["v"] for s in chunks] + [s["pieces"][2] for s in chunks] + rest,
    )[0]
    return (filtered.reshape(orbitals.shape), gram)


def solution(mesh):
    return jax.shard_map(
        shards,
        mesh=mesh,
        in_specs=(
            P("grid", None, None, "band"),
            P("grid", None, None),
            P("grid", None, None, None),
            P("grid", None),
            P(),
        ),
        out_specs=(P("grid", None, None, "band"), P("band", None)),
        check_vma=False,
    )
```

```python
import functools

import jax
import jax.numpy as jnp
import ml_dtypes
import numpy as np
from jax import lax
from jax.experimental import pallas as pl
from jax.experimental.pallas import tpu as pltpu
from jax.sharding import PartitionSpec as P

DEGREE = 4
REACH = 6
LANES = 128
QUARTER = 32

WEIGHTS = (
    -5369.0 / 1800.0,
    12.0 / 7.0,
    -15.0 / 56.0,
    10.0 / 189.0,
    -1.0 / 112.0,
    2.0 / 1925.0,
    -1.0 / 16632.0,
)
LOWER = -4.0
CUTOFF = 1.0
UPPER = 16.0
F32 = jnp.float32
BF16 = jnp.bfloat16


def filter_terms(degree):
    half_span = (UPPER - CUTOFF) / 2.0
    middle = (UPPER + CUTOFF) / 2.0
    sigma_now = half_span / (LOWER - middle)
    sigma_first = sigma_now
    scales = [sigma_now / half_span]
    recall = [0.0]
    for level in range(1, degree):
        sigma_next = 1.0 / (2.0 / sigma_first - sigma_now)
        scales.append(2.0 * sigma_next / half_span)
        recall.append(sigma_now * sigma_next)
        sigma_now = sigma_next
    return (middle, scales, recall)


def plane_matrix(ny, nz):
    def ring(n):
        m = np.zeros((n, n))
        for i in range(n):
            m[i, i] += WEIGHTS[0]
            for r in range(1, REACH + 1):
                m[i, (i + r) % n] += WEIGHTS[r]
                m[i, (i - r) % n] += WEIGHTS[r]
        return m

    full = -0.5 * (np.kron(ring(ny), np.eye(nz)) + np.kron(np.eye(ny), ring(nz)))
    high = full.astype(ml_dtypes.bfloat16)
    low = (full - high.astype(np.float64)).astype(ml_dtypes.bfloat16)
    return high, low


def halves(value):
    high = value.astype(BF16)
    return high, (value - high.astype(F32)).astype(BF16)


def dot3(*pairs):
    left, right = [], []
    for (a_high, a_low), (b_high, b_low) in pairs:
        left += [a_high, a_high, a_low]
        right += [b_high, b_low, b_high]
    return lax.dot_general(
        jnp.concatenate(left, axis=1),
        jnp.concatenate(right, axis=0),
        (((1,), (0,)), ((), ())),
        preferred_element_type=F32,
    )


def lane_ids(shape):
    return lax.broadcasted_iota(jnp.int32, shape, len(shape) - 1)


def turn(value, shift):
    if isinstance(shift, int):
        shift = shift % LANES
        if shift == 0:
            return value
    else:
        shift = lax.rem(shift + 8 * LANES, LANES)
    return pltpu.roll(value, shift, axis=value.ndim - 1)


def pack_kernel(chunk, y_ref, x_ref, *refs):
    y = y_ref[0]
    out_ref = refs[-1]
    cells = x_ref.shape[1]
    group = lane_ids((cells, LANES)) // QUARTER
    if len(refs) > 1:
        out_ref[3 * cells :] = refs[0][...]
    for r in range(3):
        row = None
        for slot, plane in enumerate((r, r + 6, r + 3, r + 9)):
            piece = turn(x_ref[plane], QUARTER * slot - 64 - QUARTER * chunk + 64 * y)
            row = piece if row is None else jnp.where(group == slot, piece, row)
        out_ref[r * cells : (r + 1) * cells] = row


def rim_pack(row, out_ref, r, source):
    part = row.shape[0] // 4
    group = lane_ids((part, LANES)) // QUARTER
    packed = None
    for j in range(4):
        piece = turn(row[j * part : (j + 1) * part], QUARTER * (j - source))
        packed = piece if packed is None else jnp.where(group == j, piece, packed)
    out_ref[pl.ds(r * part, part), :] = packed


def assemble_kernel(chunk, y_ref, x_ref, got_ref, *refs):
    y = y_ref[0]
    mh_ref, ml_ref, v_ref, up_ref, down_ref, coef_ref = refs
    cells = x_ref.shape[1]
    group = lane_ids((cells, LANES)) // QUARTER
    coef = None
    for r in range(6):
        first = turn(x_ref[r], -QUARTER * chunk)
        second = turn(x_ref[r + 6], QUARTER - QUARTER * chunk)
        other = turn(
            got_ref[cells * (r % 3) : cells * (r % 3 + 1)], 64 * (1 - y) if r < 3 else 64 * y
        )
        row = jnp.where(group == 2 * y, first, jnp.where(group == 2 * y + 1, second, other))
        v_ref[r] = row
        rim_pack(row, up_ref, r, 3)
        rim_pack(row, down_ref, r, 0)
        term = dot3(((mh_ref[r], ml_ref[r]), halves(row)))
        coef = term if coef is None else coef + term
    share_coef(coef, coef_ref, up_ref, down_ref)


def share_coef(coef, coef_ref, up_ref, down_ref):
    packed = collapse(coef)
    coef_ref[...] = packed
    rim = up_ref.shape[0] - 16
    group = lane_ids((16, LANES)) // QUARTER
    top, bottom = packed[:16], packed[16:]
    up_ref[pl.ds(rim, 16), :] = jnp.where(group % 2 == 0, turn(top, -QUARTER), bottom)
    down_ref[pl.ds(rim, 16), :] = jnp.where(group % 2 == 0, top, turn(bottom, QUARTER))


def collapse(blocks):
    group = lane_ids((32, LANES)) // QUARTER

    def block(i, s, target):
        b = 2 * i + s
        return turn(blocks[32 * b : 32 * b + 32], QUARTER * (target - i))

    low = block(0, 0, 0) + block(1, 0, 0) + block(2, 0, 0)
    high = block(1, 1, 1) + block(2, 1, 1) + block(3, 1, 1)
    below, above = block(0, 1, 2), block(3, 0, 3)
    return jnp.where(
        group == 0, low, jnp.where(group == 1, high, jnp.where(group == 2, below, above))
    )


def level_kernel(scale, recall, first, last, *refs):
    refs = list(refs)
    if last:
        yx_ref = refs.pop(0)
    v_ref = refs.pop(0)
    prev_ref = None if first else refs.pop(0)
    below_ref, above_ref = refs.pop(0), refs.pop(0)
    own_ref, kb_ref, ch_ref, cl_ref, th_ref, tl_ref, pot_ref = refs[:7]
    refs = refs[7:]
    if last:
        out_ref, own_piece, y_piece, x_piece, d_piece, ext = refs
    else:
        mh_ref, ml_ref, out_ref, up_ref, down_ref, coef_ref, ext = refs
    cells = v_ref.shape[1]
    part = cells // 4
    rim = 6 * part
    part_group = lane_ids((part, LANES)) // QUARTER
    cg = lane_ids((32, LANES)) // QUARTER
    low, high = below_ref[pl.ds(rim, 16), :], above_ref[pl.ds(rim, 16), :]
    from_below = jnp.concatenate([turn(low, 2 * QUARTER), turn(low, QUARTER)], axis=0)
    from_above = jnp.concatenate([turn(high, -QUARTER), turn(high, 2 * QUARTER)], axis=0)
    total = own_ref[...] + jnp.where(cg % 2 == 0, from_below, from_above)
    total = total * kb_ref[...]
    rows = []
    for i, s, source in (
        (0, 0, 0), (0, 1, 2), (1, 0, 0), (1, 1, 1), (2, 0, 0), (2, 1, 1), (3, 0, 3), (3, 1, 1),
    ):
        rows.append(jnp.where(cg == i, turn(total, QUARTER * (i - source)), 0.0))
    spread = halves(jnp.concatenate(rows, axis=0))
    for r in range(6):
        row = v_ref[r]
        ext[6 + r] = row
        before, after = turn(row, QUARTER), turn(row, -QUARTER)
        low, high = below_ref[pl.ds(r * part, part), :], above_ref[pl.ds(r * part, part), :]
        for j in range(4):
            cut = slice(j * part, (j + 1) * part)
            ext[r, cut] = jnp.where(part_group == 0, turn(low, -QUARTER * j), before[cut])
            ext[12 + r, cut] = jnp.where(part_group == 3, turn(high, 96 - QUARTER * j), after[cut])
    coef = None
    if last:
        mine = 2 * yx_ref[0] + yx_ref[1]
    for r in range(6):
        row = ext[6 + r]
        value = dot3(
            ((ch_ref[...], cl_ref[...]), halves(row)), ((th_ref[r], tl_ref[r]), spread)
        )
        value = value + pot_ref[r] * row
        for k in range(1, REACH + 1):
            value = value + (-0.5 * WEIGHTS[k]) * (ext[6 + r + k] + ext[6 + r - k])
        value = scale * value
        if not first:
            value = value - recall * prev_ref[r]
        out_ref[r] = value
        if last:
            for flip, piece in enumerate((own_piece, x_piece, y_piece, d_piece)):
                rim_pack(value, piece, r, lax.bitwise_xor(mine, flip))
        else:
            rim_pack(value, up_ref, r, 3)
            rim_pack(value, down_ref, r, 0)
            term = dot3(((mh_ref[r], ml_ref[r]), halves(value)))
            coef = term if coef is None else coef + term
    if not last:
        share_coef(coef, coef_ref, up_ref, down_ref)


def unpack_kernel(yx_ref, v0_ref, v1_ref, y0_ref, y1_ref, o0_ref, o1_ref, out_ref):
    y, x = yx_ref[0], yx_ref[1]
    cells = v0_ref.shape[1]
    part = cells // 4
    group = lane_ids((part, LANES)) // QUARTER
    for half, pieces in ((x, (y0_ref, y1_ref)), (1 - x, (o0_ref, o1_ref))):
        for r in range(6):
            own = [turn(v_ref[r], QUARTER * (k - half)) for k, v_ref in enumerate((v0_ref, v1_ref))]
            for j in range(4):
                rows = slice(j * part, (j + 1) * part)
                block = None
                for k in range(2):
                    got = turn(
                        pieces[k][pl.ds(r * part, part), :],
                        64 * (1 - y) + QUARTER * (k - j),
                    )
                    mine = jnp.where(group == 2 * y + k, own[k][rows], got)
                    block = mine if k == 0 else jnp.where(group % 2 == 1, mine, block)
                out_ref[6 * half + r, rows] = block


def tile_kernel(y_ref, own_ref, x_ref, y_piece_ref, d_ref, out_ref):
    y = y_ref[0]
    rows = own_ref.shape[0]
    pieces = [own_ref[...], y_piece_ref[...], x_ref[...], d_ref[...]]
    group = lane_ids((rows, LANES)) // QUARTER
    for j in range(4):
        block = None
        for s, piece in enumerate(pieces):
            target = 2 * (s // 2) + lax.bitwise_xor(y, s % 2)
            turned = turn(piece, QUARTER * (target - j))
            block = turned if block is None else jnp.where(group == target, turned, block)
        out_ref[pl.ds(j * rows, rows), :] = block


def gram_kernel(
    y_ref, a0_ref, a1_ref, s0_ref, s1_ref, own_ref, to_y_ref, to_x_ref, to_d_ref, parts_ref
):
    def dot(p, q):
        return lax.dot_general(p, q, (((0,), (0,)), ((), ())), preferred_element_type=F32)

    parts = [halves(ref[...]) for ref in (a0_ref, a1_ref, s0_ref, s1_ref)]
    high = jnp.concatenate([p[0] for p in parts], axis=1)
    low = jnp.concatenate([p[1] for p in parts], axis=1)
    left_high, left_low = high[:, :256], low[:, :256]
    total = dot(left_high, high) + (dot(left_high, low) + dot(left_low, high))
    group = lane_ids((32, LANES)) // QUARTER
    for x_row in range(2):
        for h_row in range(2):
            for k_row in range(2):
                at = 128 * k_row + 64 * x_row + 32 * h_row
                for flip in range(4):
                    x_col, core = flip // 2, flip % 2
                    block = None
                    for h in range(2):
                        for k in range(2):
                            start = 256 * core + 128 * k
                            tile = total[at : at + 32, start : start + 128]
                            piece = turn(tile, QUARTER * (2 * h + k - 2 * x_col - h))
                            block = (
                                piece
                                if block is None
                                else jnp.where(group == 2 * h + k, piece, block)
                            )
                    to = 2 * (x_col ^ x_row) + core
                    rows = slice(32 * k_row, 32 * k_row + 32)
                    parts_ref[2 * x_row + h_row, rows, 128 * to : 128 * to + 128] = block
    y = y_ref[0]
    own_ref[...] = parts_ref[y]
    to_y_ref[...] = parts_ref[1 - y]
    to_x_ref[...] = parts_ref[2 + y]
    to_d_ref[...] = parts_ref[3 - y]


def add_kernel(*refs):
    *terms, out_ref = refs
    out_ref[...] = (terms[0][...] + terms[1][...]) + (terms[2][...] + terms[3][...])


def ring_add_kernel(factor, z_ref, *refs):
    *terms, out_ref, slots = refs
    count = len(terms)
    for k, term in enumerate(terms):
        slots[lax.rem(z_ref[0] - k + count, count)] = term[...]
    total = slots[0]
    for k in range(1, count):
        total = total + slots[k]
    out_ref[...] = total * factor


def scale_kernel(factor, in_ref, out_ref):
    out_ref[...] = in_ref[...] * factor


def order_kernel(yb_ref, mine_ref, got_ref, out_ref):
    y, b = yb_ref[0], yb_ref[1]
    half = mine_ref.shape[0]
    for ref, h in ((mine_ref, y), (got_ref, 1 - y)):
        rows = pl.ds(pl.multiple_of(half * h, half), half)
        for j in range(4):
            to = pl.multiple_of(lax.bitwise_xor(b, j) * 128, 128)
            out_ref[rows, pl.ds(to, 128)] = ref[:, j * 128 : (j + 1) * 128]


def dense_kernel(yc_ref, planes_ref, proj_ref, e_ref, part_ref, rim_ref):
    y, c = yc_ref[0], yc_ref[1]
    e_ref[...] = jnp.zeros_like(e_ref)
    atoms, span, count, _ = proj_ref.shape
    for a in range(atoms):
        for b in range(span):
            at = (planes_ref[a, b], slice(a * count, (a + 1) * count))
            e_ref[at] = e_ref[at] + proj_ref[a, b]
    rows = pl.ds(pl.multiple_of(16 * c, 16), 16)
    for r in range(18):
        part_ref[r] = e_ref[6 * (1 - y) + r, rows, :]
    rim_ref[...] = e_ref[pl.ds(18 * y, 6), rows, :]


def potential_kernel(offset, y_ref, own_ref, got_ref, out_ref):
    y = y_ref[0]
    cells = out_ref.shape[1]
    own = own_ref[...] + offset
    other = got_ref[3 * cells :] + offset
    first, second = jnp.where(y == 0, own, other), jnp.where(y == 0, other, own)
    whole = jnp.concatenate([first, second], axis=0)
    fill = jnp.zeros((LANES - whole.shape[0], LANES), F32)
    columns = jnp.concatenate([whole, fill], axis=0).T
    each = cells // LANES
    group = lane_ids((LANES, LANES)) // QUARTER
    for r in range(6):
        for h in range(each):
            row = None
            for i in range(4):
                at = (6 * i + r) * each + h
                piece = jnp.broadcast_to(columns[:, at : at + 1], (LANES, LANES))
                row = piece if row is None else jnp.where(group == i, piece, row)
            out_ref[r, h * LANES : (h + 1) * LANES] = row


def gather_kernel(y_ref, part_ref, a_ref, b_ref, out_ref):
    y = y_ref[0]
    out_ref[:18] = part_ref[...]
    for r in range(6):
        one, two = a_ref[r], b_ref[r]
        out_ref[18 + r] = jnp.where(y == 1, one, two)
        out_ref[24 + r] = jnp.where(y == 1, two, one)


def maps_kernel(yc_ref, e_ref, part_ref, part2_ref, mh_ref, ml_ref, th_ref, tl_ref):
    y, c = yc_ref[0], yc_ref[1]

    def whole(plane):
        mine, rest = part_ref[plane], part2_ref[plane]
        first, second = jnp.where(c == 0, mine, rest), jnp.where(c == 0, rest, mine)
        return jnp.concatenate([first, second], axis=0)

    for r in range(6):
        below, above = whole(18 + r), whole(24 + r)
        other = [whole(6 * i + r) for i in range(3)]
        low = [jnp.where(y == 0, e_ref[6 + 6 * i + r], other[i]) for i in range(3)]
        high = [jnp.where(y == 1, e_ref[6 * i + r], other[i]) for i in range(3)]
        block = jnp.concatenate(
            [low[0], below, low[1], high[0], low[2], high[1], above, high[2]], axis=0
        )
        mh_ref[r], ml_ref[r] = halves(block)
        th_ref[r], tl_ref[r] = halves(block.T)


SMEM = pl.BlockSpec(memory_space=pltpu.SMEM)
VMEM = pl.BlockSpec(memory_space=pltpu.VMEM)
ANY = pl.BlockSpec(memory_space=pl.ANY)


def call(kernel, out, scalars, arrays, scratch=(), after=()):
    used = len(scalars) + len(arrays)

    def body(*refs):
        kernel(*refs[:used], *refs[used + len(after) :])

    return pl.pallas_call(
        body,
        out_shape=out,
        in_specs=[SMEM] * len(scalars) + [VMEM] * len(arrays) + [ANY] * len(after),
        out_specs=[VMEM] * len(out),
        scratch_shapes=list(scratch),
        compiler_params=pltpu.CompilerParams(vmem_limit_bytes=16 * 1024 * 1024),
        cost_estimate=pl.CostEstimate(flops=1 << 10, bytes_accessed=1 << 10, transcendentals=0),
    )(*scalars, *arrays, *after)


def f32(*shape):
    return pltpu.VMEM(shape, F32)


def bf16(*shape):
    return pltpu.VMEM(shape, BF16)


def shards(orbitals, potential, projectors, atom_planes, kb_energy):
    slab, ny, nz, orb_here = orbitals.shape
    cells = ny * nz
    peers = lax.axis_size("grid")
    bands = lax.axis_size("band")
    g, b = lax.axis_index("grid"), lax.axis_index("band")
    y, c, x = lax.rem(g, 2), lax.rem(b, 2), b // 2
    y1 = y.reshape(1).astype(jnp.int32)
    z1 = (g // 2).reshape(1).astype(jnp.int32)
    yb = jnp.stack([y, b]).astype(jnp.int32)
    yc = jnp.stack([y, c]).astype(jnp.int32)
    yx = jnp.stack([y, x]).astype(jnp.int32)

    def move(array, axis, target):
        size = lax.axis_size(axis)
        return lax.ppermute(array, axis, [(i, target(i) % size) for i in range(size)])

    def partner(array):
        return move(array, "grid", lambda i: i ^ 1)

    def up(array):
        return move(array, "grid", lambda i: i + 2)

    def down(array):
        return move(array, "grid", lambda i: i - 2)

    def sibling(array):
        return move(array, "band", lambda i: i ^ 1)

    def across(array):
        return move(array, "band", lambda i: i ^ 2)

    field = orbitals.reshape(slab, cells, orb_here)
    rim_rows = 6 * (cells // 4)
    middle, scales, recall = filter_terms(DEGREE)

    def diagonal(array):
        size = peers * bands
        flip = 2 * peers + 1
        return lax.ppermute(array, ("band", "grid"), [(i, i ^ flip) for i in range(size)])

    pot_own = potential.reshape(slab * cells // LANES, LANES)
    pot_rows = pot_own.shape[0]
    sent0 = call(
        functools.partial(pack_kernel, 0), [f32(3 * cells, LANES)], [y1], [field]
    )[0]
    other0 = partner(sent0)
    dense, part, rim = call(
        dense_kernel,
        [f32(24, 32, cells), f32(18, 16, cells), f32(6, 16, cells)],
        [yc, atom_planes],
        [projectors.transpose(0, 2, 1, 3)],
        after=[sent0],
    )
    part = partner(part)
    rim_a = move(rim, "grid", lambda i: i + 2 if i % 2 else i - 2)
    rim_b = move(rim, "grid", lambda i: i + 1 if i % 2 else i - 1)
    sent1 = call(
        functools.partial(pack_kernel, 1),
        [f32(3 * cells + pot_rows, LANES)],
        [y1],
        [field, pot_own],
        after=[other0],
    )[0]
    other1 = partner(sent1)
    part = call(
        gather_kernel, [f32(30, 16, cells)], [y1], [part, rim_a, rim_b], after=[sent1]
    )[0]
    mh, ml, th, tl = call(
        maps_kernel,
        [bf16(6, 256, cells)] * 2 + [bf16(6, cells, 256)] * 2,
        [yc],
        [dense, part, sibling(part)],
    )
    pot = call(
        functools.partial(potential_kernel, -(middle + 0.5 * WEIGHTS[0])),
        [f32(6, cells, LANES)],
        [y1],
        [pot_own, other1],
    )[0]
    kb = jnp.broadcast_to(jnp.tile(kb_energy, 4)[:, None], (32, LANES))
    ch, cl = (jnp.asarray(m) for m in plane_matrix(ny, nz))

    chunks = []
    for k, got in enumerate((other0, other1)):
        made = call(
            functools.partial(assemble_kernel, k),
            [f32(6, cells, LANES)] + [f32(rim_rows + 16, LANES)] * 2 + [f32(32, LANES)],
            [y1],
            [field, got, mh, ml],
        )
        chunks.append(
            dict(v=made[0], prev=None, below=up(made[1]), above=down(made[2]), coef=made[3])
        )

    for level in range(DEGREE):
        first, last = level == 0, level == DEGREE - 1
        for s in chunks:
            arrays = [s["v"]] + ([] if first else [s["prev"]]) + [s["below"], s["above"]]
            arrays += [s["coef"], kb, ch, cl, th, tl, pot]
            out = [f32(6, cells, LANES)]
            if last:
                out += [f32(rim_rows, LANES)] * 4
            else:
                arrays += [mh, ml]
                out += [f32(rim_rows + 16, LANES)] * 2 + [f32(32, LANES)]
            made = call(
                functools.partial(level_kernel, scales[level], recall[level], first, last),
                out,
                [yx] if last else [],
                arrays,
                [pltpu.VMEM((18, cells, LANES), F32)],
            )
            s["prev"], s["v"] = s["v"], made[0]
            if last:
                s["pieces"] = [made[1], across(made[3]), partner(made[2]), diagonal(made[4])]
                s["rest"] = made[4]
            else:
                s["coef"], s["below"], s["above"] = made[3], up(made[1]), down(made[2])

    tiles = [
        call(tile_kernel, [f32(4 * rim_rows, LANES)], [y1], s["pieces"])[0] for s in chunks
    ]
    quarters = call(
        gram_kernel,
        [f32(64, bands * 128)] * 4,
        [y1],
        tiles + [sibling(t) for t in tiles],
        [pltpu.VMEM((4, 64, bands * 128), F32)],
    )
    partial = call(
        add_kernel,
        [f32(64, bands * 128)],
        [],
        [quarters[0], partner(quarters[1]), across(quarters[2]), diagonal(quarters[3])],
    )[0]
    rest0, rest1, partial = lax.optimization_barrier(
        (chunks[0]["rest"], chunks[1]["rest"], partial)
    )
    rest = [partner(rest0), partner(rest1)]
    factor = 1.0 / (slab * cells * peers)
    pairs = peers // 2
    if pairs <= 4:
        moved = [partial]
        for k in range(1, pairs):
            moved.append(move(partial, "grid", lambda i, k=k: i + 2 * k))
        total = call(
            functools.partial(ring_add_kernel, factor),
            [f32(64, bands * 128)],
            [z1],
            moved,
            [pltpu.VMEM((pairs, 64, bands * 128), F32)],
            after=rest,
        )[0]
    else:
        groups = [[2 * i + j for i in range(pairs)] for j in range(2)]
        total = lax.psum(partial, "grid", axis_index_groups=groups)
        total = call(
            functools.partial(scale_kernel, factor), [f32(64, bands * 128)], [], [total]
        )[0]
    gram = call(
        order_kernel,
        [jax.ShapeDtypeStruct((128, bands * 128), F32)],
        [yb],
        [total, partner(total)],
    )[0]
    filtered = call(
        unpack_kernel,
        [jax.ShapeDtypeStruct((slab, cells, LANES), F32)],
        [yx],
        [s["v"] for s in chunks] + [s["pieces"][2] for s in chunks] + rest,
    )[0]
    return (filtered.reshape(orbitals.shape), gram)


def solution(mesh):
    return jax.shard_map(
        shards,
        mesh=mesh,
        in_specs=(
            P("grid", None, None, "band"),
            P("grid", None, None),
            P("grid", None, None, None),
            P("grid", None),
            P(),
        ),
        out_specs=(P("grid", None, None, "band"), P("band", None)),
        check_vma=False,
    )
```

```python
import functools

import jax
import jax.numpy as jnp
import ml_dtypes
import numpy as np
from jax import lax
from jax.experimental import pallas as pl
from jax.experimental.pallas import tpu as pltpu
from jax.sharding import PartitionSpec as P

DEGREE = 4
REACH = 6
LANES = 128
QUARTER = 32

WEIGHTS = (
    -5369.0 / 1800.0,
    12.0 / 7.0,
    -15.0 / 56.0,
    10.0 / 189.0,
    -1.0 / 112.0,
    2.0 / 1925.0,
    -1.0 / 16632.0,
)
LOWER = -4.0
CUTOFF = 1.0
UPPER = 16.0
F32 = jnp.float32
BF16 = jnp.bfloat16


def filter_terms(degree):
    half_span = (UPPER - CUTOFF) / 2.0
    middle = (UPPER + CUTOFF) / 2.0
    sigma_now = half_span / (LOWER - middle)
    sigma_first = sigma_now
    scales = [sigma_now / half_span]
    recall = [0.0]
    for level in range(1, degree):
        sigma_next = 1.0 / (2.0 / sigma_first - sigma_now)
        scales.append(2.0 * sigma_next / half_span)
        recall.append(sigma_now * sigma_next)
        sigma_now = sigma_next
    return (middle, scales, recall)


def plane_matrix(ny, nz):
    def ring(n):
        m = np.zeros((n, n))
        for i in range(n):
            m[i, i] += WEIGHTS[0]
            for r in range(1, REACH + 1):
                m[i, (i + r) % n] += WEIGHTS[r]
                m[i, (i - r) % n] += WEIGHTS[r]
        return m

    full = -0.5 * (np.kron(ring(ny), np.eye(nz)) + np.kron(np.eye(ny), ring(nz)))
    high = full.astype(ml_dtypes.bfloat16)
    low = (full - high.astype(np.float64)).astype(ml_dtypes.bfloat16)
    return high, low


def halves(value):
    high = value.astype(BF16)
    return high, (value - high.astype(F32)).astype(BF16)


def dot3(*pairs):
    left, right = [], []
    for (a_high, a_low), (b_high, b_low) in pairs:
        left += [a_high, a_high, a_low]
        right += [b_high, b_low, b_high]
    return lax.dot_general(
        jnp.concatenate(left, axis=1),
        jnp.concatenate(right, axis=0),
        (((1,), (0,)), ((), ())),
        preferred_element_type=F32,
    )


def dot3t(a, b):
    return lax.dot_general(
        jnp.concatenate([a[0], a[0], a[1]], axis=0),
        jnp.concatenate([b[0], b[1], b[0]], axis=0),
        (((0,), (0,)), ((), ())),
        preferred_element_type=F32,
    )


def lane_ids(shape):
    return lax.broadcasted_iota(jnp.int32, shape, len(shape) - 1)


def turn(value, shift):
    if isinstance(shift, int):
        shift = shift % LANES
        if shift == 0:
            return value
    else:
        shift = lax.rem(shift + 8 * LANES, LANES)
    return pltpu.roll(value, shift, axis=value.ndim - 1)


def pack_kernel(chunk, y_ref, x_ref, *refs):
    y = y_ref[0]
    out_ref = refs[-1]
    cells = x_ref.shape[1]
    group = lane_ids((cells, LANES)) // QUARTER
    if len(refs) > 1:
        out_ref[3 * cells :] = refs[0][...]
    for r in range(3):
        row = None
        for slot, plane in enumerate((r, r + 6, r + 3, r + 9)):
            piece = turn(x_ref[plane], QUARTER * slot - 64 - QUARTER * chunk + 64 * y)
            row = piece if row is None else jnp.where(group == slot, piece, row)
        out_ref[r * cells : (r + 1) * cells] = row


def rim_pack(row, out_ref, r, source):
    part = row.shape[0] // 4
    group = lane_ids((part, LANES)) // QUARTER
    packed = None
    for j in range(4):
        piece = turn(row[j * part : (j + 1) * part], QUARTER * (j - source))
        packed = piece if packed is None else jnp.where(group == j, piece, packed)
    out_ref[pl.ds(r * part, part), :] = packed


def assemble_kernel(chunk, y_ref, x_ref, got_ref, *refs):
    y = y_ref[0]
    mh_ref, ml_ref, v_ref, up_ref, down_ref, coef_ref = refs
    cells = x_ref.shape[1]
    group = lane_ids((cells, LANES)) // QUARTER
    coef = None
    for r in range(6):
        first = turn(x_ref[r], -QUARTER * chunk)
        second = turn(x_ref[r + 6], QUARTER - QUARTER * chunk)
        other = turn(
            got_ref[cells * (r % 3) : cells * (r % 3 + 1)], 64 * (1 - y) if r < 3 else 64 * y
        )
        row = jnp.where(group == 2 * y, first, jnp.where(group == 2 * y + 1, second, other))
        v_ref[r] = row
        rim_pack(row, up_ref, r, 3)
        rim_pack(row, down_ref, r, 0)
        term = dot3(((mh_ref[r], ml_ref[r]), halves(row)))
        coef = term if coef is None else coef + term
    share_coef(coef, coef_ref, up_ref, down_ref)


def share_coef(coef, coef_ref, up_ref, down_ref):
    packed = collapse(coef)
    coef_ref[...] = packed
    rim = up_ref.shape[0] - 16
    group = lane_ids((16, LANES)) // QUARTER
    top, bottom = packed[:16], packed[16:]
    up_ref[pl.ds(rim, 16), :] = jnp.where(group % 2 == 0, turn(top, -QUARTER), bottom)
    down_ref[pl.ds(rim, 16), :] = jnp.where(group % 2 == 0, top, turn(bottom, QUARTER))


def collapse(blocks):
    group = lane_ids((32, LANES)) // QUARTER

    def block(i, s, target):
        b = 2 * i + s
        return turn(blocks[32 * b : 32 * b + 32], QUARTER * (target - i))

    low = block(0, 0, 0) + block(1, 0, 0) + block(2, 0, 0)
    high = block(1, 1, 1) + block(2, 1, 1) + block(3, 1, 1)
    below, above = block(0, 1, 2), block(3, 0, 3)
    return jnp.where(
        group == 0, low, jnp.where(group == 1, high, jnp.where(group == 2, below, above))
    )


def level_kernel(scale, recall, first, last, *refs):
    refs = list(refs)
    if last:
        yx_ref = refs.pop(0)
    v_ref = refs.pop(0)
    prev_ref = None if first else refs.pop(0)
    below_ref, above_ref = refs.pop(0), refs.pop(0)
    own_ref, kb_ref, ch_ref, cl_ref, pot_ref, mh_ref, ml_ref = refs[:7]
    refs = refs[7:]
    if last:
        own_piece, y_piece, x_piece, d_piece, ext = refs
    else:
        out_ref, up_ref, down_ref, coef_ref, ext = refs
    cells = v_ref.shape[1]
    part = cells // 4
    rim = 6 * part
    part_group = lane_ids((part, LANES)) // QUARTER
    cg = lane_ids((32, LANES)) // QUARTER
    low, high = below_ref[pl.ds(rim, 16), :], above_ref[pl.ds(rim, 16), :]
    from_below = jnp.concatenate([turn(low, 2 * QUARTER), turn(low, QUARTER)], axis=0)
    from_above = jnp.concatenate([turn(high, -QUARTER), turn(high, 2 * QUARTER)], axis=0)
    total = own_ref[...] + jnp.where(cg % 2 == 0, from_below, from_above)
    total = total * kb_ref[...]
    rows = []
    for i, s, source in (
        (0, 0, 0), (0, 1, 2), (1, 0, 0), (1, 1, 1), (2, 0, 0), (2, 1, 1), (3, 0, 3), (3, 1, 1),
    ):
        rows.append(jnp.where(cg == i, turn(total, QUARTER * (i - source)), 0.0))
    spread = halves(jnp.concatenate(rows, axis=0))
    for r in range(6):
        row = v_ref[r]
        ext[6 + r] = row
        before, after = turn(row, QUARTER), turn(row, -QUARTER)
        low, high = below_ref[pl.ds(r * part, part), :], above_ref[pl.ds(r * part, part), :]
        for j in range(4):
            cut = slice(j * part, (j + 1) * part)
            ext[r, cut] = jnp.where(part_group == 0, turn(low, -QUARTER * j), before[cut])
            ext[12 + r, cut] = jnp.where(part_group == 3, turn(high, 96 - QUARTER * j), after[cut])
    coef = None
    if last:
        mine = 2 * yx_ref[0] + yx_ref[1]
    for r in range(6):
        row = ext[6 + r]
        value = dot3(((ch_ref[...], cl_ref[...]), halves(row)))
        value = value + dot3t((mh_ref[r], ml_ref[r]), spread)
        value = value + pot_ref[r] * row
        for k in range(1, REACH + 1):
            value = value + (-0.5 * WEIGHTS[k]) * (ext[6 + r + k] + ext[6 + r - k])
        value = scale * value
        if not first:
            value = value - recall * prev_ref[r]
        if last:
            for flip, piece in enumerate((own_piece, x_piece, y_piece, d_piece)):
                rim_pack(value, piece, r, lax.bitwise_xor(mine, flip))
        else:
            out_ref[r] = value
            rim_pack(value, up_ref, r, 3)
            rim_pack(value, down_ref, r, 0)
            term = dot3(((mh_ref[r], ml_ref[r]), halves(value)))
            coef = term if coef is None else coef + term
    if not last:
        share_coef(coef, coef_ref, up_ref, down_ref)


def unpack_kernel(
    yx_ref, own0_ref, own1_ref, x0_ref, x1_ref, y0_ref, y1_ref, rest_ref, out_ref
):
    y, x = yx_ref[0], yx_ref[1]
    cells = out_ref.shape[1]
    part = cells // 4
    rim = 6 * part
    group = lane_ids((part, LANES)) // QUARTER
    rest = [rest_ref.at[pl.ds(k * rim, rim)] for k in range(2)]
    for half, own, got in (
        (x, (own0_ref, own1_ref), (y0_ref, y1_ref)),
        (1 - x, (x0_ref, x1_ref), rest),
    ):
        for r in range(6):
            for j in range(4):
                block = None
                for k in range(2):
                    here = turn(own[k][pl.ds(r * part, part), :], 64 * y + QUARTER * (k - j))
                    there = turn(got[k][pl.ds(r * part, part), :], 64 * (1 - y) + QUARTER * (k - j))
                    mine = jnp.where(group == 2 * y + k, here, there)
                    block = mine if k == 0 else jnp.where(group % 2 == 1, mine, block)
                out_ref[6 * half + r, j * part : (j + 1) * part] = block


def tile_kernel(y_ref, own_ref, x_ref, y_piece_ref, d_ref, *refs):
    y = y_ref[0]
    rows = own_ref.shape[0]
    out_ref = refs[2] if len(refs) > 2 else refs[0]
    if len(refs) > 2:
        refs[3][:rows] = refs[0][...]
        refs[3][rows:] = refs[1][...]
    pieces = [own_ref[...], y_piece_ref[...], x_ref[...], d_ref[...]]
    group = lane_ids((rows, LANES)) // QUARTER
    for j in range(4):
        block = None
        for s, piece in enumerate(pieces):
            target = 2 * (s // 2) + lax.bitwise_xor(y, s % 2)
            turned = turn(piece, QUARTER * (target - j))
            block = turned if block is None else jnp.where(group == target, turned, block)
        out_ref[pl.ds(j * rows, rows), :] = block


def gram_product(left, right):
    def dot(p, q):
        return lax.dot_general(p, q, (((0,), (0,)), ((), ())), preferred_element_type=F32)

    def side(parts, i):
        return jnp.concatenate([p[i] for p in parts], axis=1)

    high, low = side(left, 0), side(left, 1)
    return dot(high, side(right, 0)) + (dot(high, side(right, 1)) + dot(low, side(right, 0)))


def gram_early_kernel(a0_ref, a1_ref, s0_ref, out_ref):
    parts = [halves(ref[...]) for ref in (a0_ref, a1_ref, s0_ref)]
    out_ref[...] = gram_product(parts[:2], parts)


def gram_kernel(
    y_ref, a0_ref, a1_ref, s1_ref, early_ref, own_ref, to_y_ref, to_x_ref, to_d_ref, parts_ref
):
    parts = [halves(ref[...]) for ref in (a0_ref, a1_ref, s1_ref)]
    late = gram_product(parts[:2], parts[2:])
    total = jnp.concatenate([early_ref[...], late], axis=1)
    group = lane_ids((32, LANES)) // QUARTER
    for x_row in range(2):
        for h_row in range(2):
            for k_row in range(2):
                at = 128 * k_row + 64 * x_row + 32 * h_row
                for flip in range(4):
                    x_col, core = flip // 2, flip % 2
                    block = None
                    for h in range(2):
                        for k in range(2):
                            start = 256 * core + 128 * k
                            tile = total[at : at + 32, start : start + 128]
                            piece = turn(tile, QUARTER * (2 * h + k - 2 * x_col - h))
                            block = (
                                piece
                                if block is None
                                else jnp.where(group == 2 * h + k, piece, block)
                            )
                    to = 2 * (x_col ^ x_row) + core
                    rows = slice(32 * k_row, 32 * k_row + 32)
                    parts_ref[2 * x_row + h_row, rows, 128 * to : 128 * to + 128] = block
    y = y_ref[0]
    own_ref[...] = parts_ref[y]
    to_y_ref[...] = parts_ref[1 - y]
    to_x_ref[...] = parts_ref[2 + y]
    to_d_ref[...] = parts_ref[3 - y]


def add_kernel(*refs):
    *terms, out_ref = refs
    out_ref[...] = (terms[0][...] + terms[1][...]) + (terms[2][...] + terms[3][...])


def ring_add_kernel(factor, z_ref, *refs):
    *terms, out_ref, slots = refs
    count = len(terms)
    for k, term in enumerate(terms):
        slots[lax.rem(z_ref[0] - k + count, count)] = term[...]
    total = slots[0]
    for k in range(1, count):
        total = total + slots[k]
    out_ref[...] = total * factor


def scale_kernel(factor, in_ref, out_ref):
    out_ref[...] = in_ref[...] * factor


def order_kernel(yb_ref, mine_ref, got_ref, out_ref):
    y, b = yb_ref[0], yb_ref[1]
    half = mine_ref.shape[0]
    for ref, h in ((mine_ref, y), (got_ref, 1 - y)):
        rows = pl.ds(pl.multiple_of(half * h, half), half)
        for j in range(4):
            to = pl.multiple_of(lax.bitwise_xor(b, j) * 128, 128)
            out_ref[rows, pl.ds(to, 128)] = ref[:, j * 128 : (j + 1) * 128]


def dense_kernel(yc_ref, planes_ref, proj_ref, pot_ref, e_ref, part_ref, rim_ref):
    y, c = yc_ref[0], yc_ref[1]
    e_ref[...] = jnp.zeros_like(e_ref)
    atoms, span, count, _ = proj_ref.shape
    for a in range(atoms):
        for b in range(span):
            at = (planes_ref[a, b], slice(a * count, (a + 1) * count))
            e_ref[at] = e_ref[at] + proj_ref[a, b]
    rows = pl.ds(pl.multiple_of(16 * c, 16), 16)
    for r in range(18):
        part_ref[r] = e_ref[6 * (1 - y) + r, rows, :]
    part_ref[18] = jnp.zeros(part_ref.shape[1:], F32)
    part_ref[18, : pot_ref.shape[0]] = pot_ref[...]
    rim_ref[...] = e_ref[pl.ds(18 * y, 6), rows, :]


def potential_kernel(offset, y_ref, own_ref, part_ref, out_ref):
    y = y_ref[0]
    own = own_ref[...] + offset
    other = part_ref[18, : own.shape[0]] + offset
    first, second = jnp.where(y == 0, own, other), jnp.where(y == 0, other, own)
    fill = jnp.zeros((8, own.shape[1]), F32)
    columns = jnp.concatenate([first, second, fill], axis=0).T
    group = lane_ids((own.shape[1], LANES)) // QUARTER
    for r in range(6):
        row = None
        for i in range(4):
            at = 6 * i + r
            piece = jnp.broadcast_to(columns[:, at : at + 1], (own.shape[1], LANES))
            row = piece if row is None else jnp.where(group == i, piece, row)
        out_ref[r] = row


def gather_kernel(y_ref, part_ref, a_ref, b_ref, out_ref):
    y = y_ref[0]
    out_ref[:18] = part_ref[:18]
    for r in range(6):
        one, two = a_ref[r], b_ref[r]
        out_ref[18 + r] = jnp.where(y == 1, one, two)
        out_ref[24 + r] = jnp.where(y == 1, two, one)


def maps_kernel(yc_ref, e_ref, part_ref, part2_ref, mh_ref, ml_ref):
    y, c = yc_ref[0], yc_ref[1]

    def whole(plane):
        mine, rest = part_ref[plane], part2_ref[plane]
        first, second = jnp.where(c == 0, mine, rest), jnp.where(c == 0, rest, mine)
        return jnp.concatenate([first, second], axis=0)

    for r in range(6):
        below, above = whole(18 + r), whole(24 + r)
        other = [whole(6 * i + r) for i in range(3)]
        low = [jnp.where(y == 0, e_ref[6 + 6 * i + r], other[i]) for i in range(3)]
        high = [jnp.where(y == 1, e_ref[6 * i + r], other[i]) for i in range(3)]
        block = jnp.concatenate(
            [low[0], below, low[1], high[0], low[2], high[1], above, high[2]], axis=0
        )
        mh_ref[r], ml_ref[r] = halves(block)


SMEM = pl.BlockSpec(memory_space=pltpu.SMEM)
VMEM = pl.BlockSpec(memory_space=pltpu.VMEM)
ANY = pl.BlockSpec(memory_space=pl.ANY)


def call(kernel, out, scalars, arrays, scratch=(), after=()):
    used = len(scalars) + len(arrays)

    def body(*refs):
        kernel(*refs[:used], *refs[used + len(after) :])

    return pl.pallas_call(
        body,
        out_shape=out,
        in_specs=[SMEM] * len(scalars) + [VMEM] * len(arrays) + [ANY] * len(after),
        out_specs=[VMEM] * len(out),
        scratch_shapes=list(scratch),
        compiler_params=pltpu.CompilerParams(vmem_limit_bytes=16 * 1024 * 1024),
        cost_estimate=pl.CostEstimate(flops=1 << 10, bytes_accessed=1 << 10, transcendentals=0),
    )(*scalars, *arrays, *after)


def f32(*shape):
    return pltpu.VMEM(shape, F32)


def bf16(*shape):
    return pltpu.VMEM(shape, BF16)


def shards(orbitals, potential, projectors, atom_planes, kb_energy):
    slab, ny, nz, orb_here = orbitals.shape
    cells = ny * nz
    peers = lax.axis_size("grid")
    bands = lax.axis_size("band")
    g, b = lax.axis_index("grid"), lax.axis_index("band")
    y, c, x = lax.rem(g, 2), lax.rem(b, 2), b // 2
    y1 = y.reshape(1).astype(jnp.int32)
    z1 = (g // 2).reshape(1).astype(jnp.int32)
    yb = jnp.stack([y, b]).astype(jnp.int32)
    yc = jnp.stack([y, c]).astype(jnp.int32)
    yx = jnp.stack([y, x]).astype(jnp.int32)

    def move(array, axis, target):
        size = lax.axis_size(axis)
        return lax.ppermute(array, axis, [(i, target(i) % size) for i in range(size)])

    def partner(array):
        return move(array, "grid", lambda i: i ^ 1)

    def up(array):
        return move(array, "grid", lambda i: i + 2)

    def down(array):
        return move(array, "grid", lambda i: i - 2)

    def sibling(array):
        return move(array, "band", lambda i: i ^ 1)

    def across(array):
        return move(array, "band", lambda i: i ^ 2)

    field = orbitals.reshape(slab, cells, orb_here)
    rim_rows = 6 * (cells // 4)
    middle, scales, recall = filter_terms(DEGREE)

    def diagonal(array):
        size = peers * bands
        flip = 2 * peers + 1
        return lax.ppermute(array, ("band", "grid"), [(i, i ^ flip) for i in range(size)])

    pot_own = potential.reshape(slab, cells)
    sent0 = call(
        functools.partial(pack_kernel, 0), [f32(3 * cells, LANES)], [y1], [field]
    )[0]
    other0 = partner(sent0)
    dense, part, rim = call(
        dense_kernel,
        [f32(24, 32, cells), f32(19, 16, cells), f32(6, 16, cells)],
        [yc, atom_planes],
        [projectors.transpose(0, 2, 1, 3), pot_own],
        after=[sent0],
    )
    part = partner(part)
    rim_a = move(rim, "grid", lambda i: i + 2 if i % 2 else i - 2)
    rim_b = move(rim, "grid", lambda i: i + 1 if i % 2 else i - 1)
    sent1 = call(
        functools.partial(pack_kernel, 1),
        [f32(3 * cells, LANES)],
        [y1],
        [field],
        after=[other0],
    )[0]
    other1 = partner(sent1)
    pot_part = part
    part = call(
        gather_kernel, [f32(30, 16, cells)], [y1], [part, rim_a, rim_b], after=[sent1]
    )[0]
    mh, ml = call(
        maps_kernel,
        [bf16(6, 256, cells)] * 2,
        [yc],
        [dense, part, sibling(part)],
    )
    pot = call(
        functools.partial(potential_kernel, -(middle + 0.5 * WEIGHTS[0])),
        [f32(6, cells, LANES)],
        [y1],
        [pot_own, pot_part],
        after=[mh],
    )[0]
    kb = jnp.broadcast_to(jnp.tile(kb_energy, 4)[:, None], (32, LANES))
    ch, cl = (jnp.asarray(m) for m in plane_matrix(ny, nz))

    chunks = []
    for k, got in enumerate((other0, other1)):
        made = call(
            functools.partial(assemble_kernel, k),
            [f32(6, cells, LANES)] + [f32(rim_rows + 16, LANES)] * 2 + [f32(32, LANES)],
            [y1],
            [field, got, mh, ml],
            after=[pot] if k else [],
        )
        chunks.append(
            dict(v=made[0], prev=None, below=up(made[1]), above=down(made[2]), coef=made[3])
        )

    for level in range(DEGREE):
        first, last = level == 0, level == DEGREE - 1
        for s in chunks:
            arrays = [s["v"]] + ([] if first else [s["prev"]]) + [s["below"], s["above"]]
            arrays += [s["coef"], kb, ch, cl, pot, mh, ml]
            if last:
                out = [f32(rim_rows, LANES)] * 4
            else:
                out = [f32(6, cells, LANES)] + [f32(rim_rows + 16, LANES)] * 2 + [f32(32, LANES)]
            made = call(
                functools.partial(level_kernel, scales[level], recall[level], first, last),
                out,
                [yx] if last else [],
                arrays,
                [pltpu.VMEM((18, cells, LANES), F32)],
            )
            if last:
                own, for_y, for_x, rest = made
                s["pieces"] = [own, across(for_x), partner(for_y), diagonal(rest)]
                s["for_x"], s["rest"] = for_x, rest
            else:
                s["prev"], s["v"] = s["v"], made[0]
                s["coef"], s["below"], s["above"] = made[3], up(made[1]), down(made[2])

    tile0, rest = call(
        tile_kernel,
        [f32(4 * rim_rows, LANES), f32(2 * rim_rows, LANES)],
        [y1],
        chunks[0]["pieces"] + [s["rest"] for s in chunks],
    )
    tile1 = call(tile_kernel, [f32(4 * rim_rows, LANES)], [y1], chunks[1]["pieces"])[0]
    early = call(
        gram_early_kernel, [f32(256, 384)], [], [tile0, tile1, sibling(tile0)]
    )[0]
    quarters = call(
        gram_kernel,
        [f32(64, bands * 128)] * 4,
        [y1],
        [tile0, tile1, sibling(tile1), early],
        [pltpu.VMEM((4, 64, bands * 128), F32)],
    )
    partial = call(
        add_kernel,
        [f32(64, bands * 128)],
        [],
        [quarters[0], partner(quarters[1]), across(quarters[2]), diagonal(quarters[3])],
    )[0]
    rest, partial = lax.optimization_barrier((rest, partial))
    rest = partner(rest)
    factor = 1.0 / (slab * cells * peers)
    pairs = peers // 2
    if pairs <= 4:
        moved = [partial]
        for k in range(1, pairs):
            moved.append(move(partial, "grid", lambda i, k=k: i + 2 * k))
        total = call(
            functools.partial(ring_add_kernel, factor),
            [f32(64, bands * 128)],
            [z1],
            moved,
            [pltpu.VMEM((pairs, 64, bands * 128), F32)],
            after=[rest],
        )[0]
    else:
        groups = [[2 * i + j for i in range(pairs)] for j in range(2)]
        total = lax.psum(partial, "grid", axis_index_groups=groups)
        total = call(
            functools.partial(scale_kernel, factor), [f32(64, bands * 128)], [], [total]
        )[0]
    gram = call(
        order_kernel,
        [jax.ShapeDtypeStruct((128, bands * 128), F32)],
        [yb],
        [total, partner(total)],
    )[0]
    filtered = call(
        unpack_kernel,
        [jax.ShapeDtypeStruct((slab, cells, LANES), F32)],
        [yx],
        [s["pieces"][0] for s in chunks]
        + [s["for_x"] for s in chunks]
        + [s["pieces"][2] for s in chunks]
        + [rest],
    )[0]
    return (filtered.reshape(orbitals.shape), gram)


def solution(mesh):
    return jax.shard_map(
        shards,
        mesh=mesh,
        in_specs=(
            P("grid", None, None, "band"),
            P("grid", None, None),
            P("grid", None, None, None),
            P("grid", None),
            P(),
        ),
        out_specs=(P("grid", None, None, "band"), P("band", None)),
        check_vma=False,
    )
```

```python
import functools

import jax
import jax.numpy as jnp
import ml_dtypes
import numpy as np
from jax import lax
from jax.experimental import pallas as pl
from jax.experimental.pallas import tpu as pltpu
from jax.sharding import PartitionSpec as P

DEGREE = 4
REACH = 6
LANES = 128
QUARTER = 32

WEIGHTS = (
    -5369.0 / 1800.0,
    12.0 / 7.0,
    -15.0 / 56.0,
    10.0 / 189.0,
    -1.0 / 112.0,
    2.0 / 1925.0,
    -1.0 / 16632.0,
)
LOWER = -4.0
CUTOFF = 1.0
UPPER = 16.0
F32 = jnp.float32
BF16 = jnp.bfloat16


def filter_terms(degree):
    half_span = (UPPER - CUTOFF) / 2.0
    middle = (UPPER + CUTOFF) / 2.0
    sigma_now = half_span / (LOWER - middle)
    sigma_first = sigma_now
    scales = [sigma_now / half_span]
    recall = [0.0]
    for level in range(1, degree):
        sigma_next = 1.0 / (2.0 / sigma_first - sigma_now)
        scales.append(2.0 * sigma_next / half_span)
        recall.append(sigma_now * sigma_next)
        sigma_now = sigma_next
    return (middle, scales, recall)


def plane_matrix(ny, nz):
    def ring(n):
        m = np.zeros((n, n))
        for i in range(n):
            m[i, i] += WEIGHTS[0]
            for r in range(1, REACH + 1):
                m[i, (i + r) % n] += WEIGHTS[r]
                m[i, (i - r) % n] += WEIGHTS[r]
        return m

    full = -0.5 * (np.kron(ring(ny), np.eye(nz)) + np.kron(np.eye(ny), ring(nz)))
    high = full.astype(ml_dtypes.bfloat16)
    low = (full - high.astype(np.float64)).astype(ml_dtypes.bfloat16)
    return high, low


def halves(value):
    high = value.astype(BF16)
    return high, (value - high.astype(F32)).astype(BF16)


def dot3(*pairs):
    left, right = [], []
    for (a_high, a_low), (b_high, b_low) in pairs:
        left += [a_high, a_high, a_low]
        right += [b_high, b_low, b_high]
    return lax.dot_general(
        jnp.concatenate(left, axis=1),
        jnp.concatenate(right, axis=0),
        (((1,), (0,)), ((), ())),
        preferred_element_type=F32,
    )


def lane_ids(shape):
    return lax.broadcasted_iota(jnp.int32, shape, len(shape) - 1)


def turn(value, shift):
    if isinstance(shift, int):
        shift = shift % LANES
        if shift == 0:
            return value
    else:
        shift = lax.rem(shift + 8 * LANES, LANES)
    return pltpu.roll(value, shift, axis=value.ndim - 1)


def pack_kernel(chunk, y_ref, x_ref, *refs):
    y = y_ref[0]
    out_ref = refs[-1]
    cells = x_ref.shape[1]
    group = lane_ids((cells, LANES)) // QUARTER
    if len(refs) > 1:
        out_ref[3 * cells :] = refs[0][...]
    for r in range(3):
        row = None
        for slot, plane in enumerate((r, r + 6, r + 3, r + 9)):
            piece = turn(x_ref[plane], QUARTER * slot - 64 - QUARTER * chunk + 64 * y)
            row = piece if row is None else jnp.where(group == slot, piece, row)
        out_ref[r * cells : (r + 1) * cells] = row


def rim_pack(row, out_ref, r, source):
    part = row.shape[0] // 4
    group = lane_ids((part, LANES)) // QUARTER
    packed = None
    for j in range(4):
        piece = turn(row[j * part : (j + 1) * part], QUARTER * (j - source))
        packed = piece if packed is None else jnp.where(group == j, piece, packed)
    out_ref[pl.ds(r * part, part), :] = packed


def assemble_kernel(chunk, y_ref, x_ref, got_ref, *refs):
    y = y_ref[0]
    mh_ref, ml_ref, v_ref, up_ref, down_ref, coef_ref = refs
    cells = x_ref.shape[1]
    group = lane_ids((cells, LANES)) // QUARTER
    coef = None
    for r in range(6):
        first = turn(x_ref[r], -QUARTER * chunk)
        second = turn(x_ref[r + 6], QUARTER - QUARTER * chunk)
        other = turn(
            got_ref[cells * (r % 3) : cells * (r % 3 + 1)], 64 * (1 - y) if r < 3 else 64 * y
        )
        row = jnp.where(group == 2 * y, first, jnp.where(group == 2 * y + 1, second, other))
        v_ref[r] = row
        rim_pack(row, up_ref, r, 3)
        rim_pack(row, down_ref, r, 0)
        term = dot3(((mh_ref[r], ml_ref[r]), halves(row)))
        coef = term if coef is None else coef + term
    share_coef(coef, coef_ref, up_ref, down_ref)


def share_coef(coef, coef_ref, up_ref, down_ref):
    packed = collapse(coef)
    coef_ref[...] = packed
    rim = up_ref.shape[0] - 16
    group = lane_ids((16, LANES)) // QUARTER
    top, bottom = packed[:16], packed[16:]
    up_ref[pl.ds(rim, 16), :] = jnp.where(group % 2 == 0, turn(top, -QUARTER), bottom)
    down_ref[pl.ds(rim, 16), :] = jnp.where(group % 2 == 0, top, turn(bottom, QUARTER))


def collapse(blocks):
    group = lane_ids((32, LANES)) // QUARTER

    def block(i, s, target):
        b = 2 * i + s
        return turn(blocks[32 * b : 32 * b + 32], QUARTER * (target - i))

    low = block(0, 0, 0) + block(1, 0, 0) + block(2, 0, 0)
    high = block(1, 1, 1) + block(2, 1, 1) + block(3, 1, 1)
    below, above = block(0, 1, 2), block(3, 0, 3)
    return jnp.where(
        group == 0, low, jnp.where(group == 1, high, jnp.where(group == 2, below, above))
    )


def level_kernel(scale, recall, first, last, *refs):
    refs = list(refs)
    if last:
        yx_ref = refs.pop(0)
    v_ref = refs.pop(0)
    prev_ref = None if first else refs.pop(0)
    below_ref, above_ref = refs.pop(0), refs.pop(0)
    own_ref, kb_ref, ch_ref, cl_ref, th_ref, tl_ref, pot_ref = refs[:7]
    refs = refs[7:]
    if last:
        own_piece, y_piece, x_piece, d_piece, ext = refs
    else:
        mh_ref, ml_ref, out_ref, up_ref, down_ref, coef_ref, ext = refs
    cells = v_ref.shape[1]
    part = cells // 4
    rim = 6 * part
    part_group = lane_ids((part, LANES)) // QUARTER
    cg = lane_ids((32, LANES)) // QUARTER
    low, high = below_ref[pl.ds(rim, 16), :], above_ref[pl.ds(rim, 16), :]
    from_below = jnp.concatenate([turn(low, 2 * QUARTER), turn(low, QUARTER)], axis=0)
    from_above = jnp.concatenate([turn(high, -QUARTER), turn(high, 2 * QUARTER)], axis=0)
    total = own_ref[...] + jnp.where(cg % 2 == 0, from_below, from_above)
    total = total * kb_ref[...]
    rows = []
    for i, s, source in (
        (0, 0, 0), (0, 1, 2), (1, 0, 0), (1, 1, 1), (2, 0, 0), (2, 1, 1), (3, 0, 3), (3, 1, 1),
    ):
        rows.append(jnp.where(cg == i, turn(total, QUARTER * (i - source)), 0.0))
    spread = halves(jnp.concatenate(rows, axis=0))
    for r in range(6):
        row = v_ref[r]
        ext[6 + r] = row
        before, after = turn(row, QUARTER), turn(row, -QUARTER)
        low, high = below_ref[pl.ds(r * part, part), :], above_ref[pl.ds(r * part, part), :]
        for j in range(4):
            cut = slice(j * part, (j + 1) * part)
            ext[r, cut] = jnp.where(part_group == 0, turn(low, -QUARTER * j), before[cut])
            ext[12 + r, cut] = jnp.where(part_group == 3, turn(high, 96 - QUARTER * j), after[cut])
    coef = None
    pot = pot_ref[...]
    if last:
        mine = 2 * yx_ref[0] + yx_ref[1]
    for r in range(6):
        row = ext[6 + r]
        value = dot3(
            ((ch_ref[...], cl_ref[...]), halves(row)), ((th_ref[r], tl_ref[r]), spread)
        )
        value = value + potential_row(pot, r) * row
        for k in range(1, REACH + 1):
            value = value + (-0.5 * WEIGHTS[k]) * (ext[6 + r + k] + ext[6 + r - k])
        value = scale * value
        if not first:
            value = value - recall * prev_ref[r]
        if last:
            for flip, piece in enumerate((own_piece, x_piece, y_piece, d_piece)):
                rim_pack(value, piece, r, lax.bitwise_xor(mine, flip))
        else:
            out_ref[r] = value
            rim_pack(value, up_ref, r, 3)
            rim_pack(value, down_ref, r, 0)
            term = dot3(((mh_ref[r], ml_ref[r]), halves(value)))
            coef = term if coef is None else coef + term
    if not last:
        share_coef(coef, coef_ref, up_ref, down_ref)


def unpack_kernel(
    yx_ref, own0_ref, own1_ref, x0_ref, x1_ref, y0_ref, y1_ref, rest_ref, out_ref
):
    y, x = yx_ref[0], yx_ref[1]
    cells = out_ref.shape[1]
    part = cells // 4
    rim = 6 * part
    group = lane_ids((part, LANES)) // QUARTER
    rest = [rest_ref.at[pl.ds(k * rim, rim)] for k in range(2)]
    for half, own, got in (
        (x, (own0_ref, own1_ref), (y0_ref, y1_ref)),
        (1 - x, (x0_ref, x1_ref), rest),
    ):
        for r in range(6):
            for j in range(4):
                block = None
                for k in range(2):
                    here = turn(own[k][pl.ds(r * part, part), :], 64 * y + QUARTER * (k - j))
                    there = turn(got[k][pl.ds(r * part, part), :], 64 * (1 - y) + QUARTER * (k - j))
                    mine = jnp.where(group == 2 * y + k, here, there)
                    block = mine if k == 0 else jnp.where(group % 2 == 1, mine, block)
                out_ref[6 * half + r, j * part : (j + 1) * part] = block


def tile_kernel(y_ref, own_ref, x_ref, y_piece_ref, d_ref, *refs):
    y = y_ref[0]
    rows = own_ref.shape[0]
    out_ref = refs[2] if len(refs) > 2 else refs[0]
    if len(refs) > 2:
        refs[3][:rows] = refs[0][...]
        refs[3][rows:] = refs[1][...]
    pieces = [own_ref[...], y_piece_ref[...], x_ref[...], d_ref[...]]
    group = lane_ids((rows, LANES)) // QUARTER
    for j in range(4):
        block = None
        for s, piece in enumerate(pieces):
            target = 2 * (s // 2) + lax.bitwise_xor(y, s % 2)
            turned = turn(piece, QUARTER * (target - j))
            block = turned if block is None else jnp.where(group == target, turned, block)
        out_ref[pl.ds(j * rows, rows), :] = block


def gram_product(left, right):
    def dot(p, q):
        return lax.dot_general(p, q, (((0,), (0,)), ((), ())), preferred_element_type=F32)

    def side(parts, i):
        return jnp.concatenate([p[i] for p in parts], axis=1)

    high, low = side(left, 0), side(left, 1)
    return dot(high, side(right, 0)) + (dot(high, side(right, 1)) + dot(low, side(right, 0)))


def gram_early_kernel(a0_ref, a1_ref, s0_ref, out_ref):
    parts = [halves(ref[...]) for ref in (a0_ref, a1_ref, s0_ref)]
    out_ref[...] = gram_product(parts[:2], parts)


def gram_kernel(
    y_ref, a0_ref, a1_ref, s1_ref, early_ref, own_ref, to_y_ref, to_x_ref, to_d_ref, parts_ref
):
    parts = [halves(ref[...]) for ref in (a0_ref, a1_ref, s1_ref)]
    late = gram_product(parts[:2], parts[2:])
    total = jnp.concatenate([early_ref[...], late], axis=1)
    group = lane_ids((32, LANES)) // QUARTER
    for x_row in range(2):
        for h_row in range(2):
            for k_row in range(2):
                at = 128 * k_row + 64 * x_row + 32 * h_row
                for flip in range(4):
                    x_col, core = flip // 2, flip % 2
                    block = None
                    for h in range(2):
                        for k in range(2):
                            start = 256 * core + 128 * k
                            tile = total[at : at + 32, start : start + 128]
                            piece = turn(tile, QUARTER * (2 * h + k - 2 * x_col - h))
                            block = (
                                piece
                                if block is None
                                else jnp.where(group == 2 * h + k, piece, block)
                            )
                    to = 2 * (x_col ^ x_row) + core
                    rows = slice(32 * k_row, 32 * k_row + 32)
                    parts_ref[2 * x_row + h_row, rows, 128 * to : 128 * to + 128] = block
    y = y_ref[0]
    own_ref[...] = parts_ref[y]
    to_y_ref[...] = parts_ref[1 - y]
    to_x_ref[...] = parts_ref[2 + y]
    to_d_ref[...] = parts_ref[3 - y]


def add_kernel(*refs):
    *terms, out_ref = refs
    out_ref[...] = (terms[0][...] + terms[1][...]) + (terms[2][...] + terms[3][...])


def ring_add_kernel(factor, z_ref, *refs):
    *terms, out_ref, slots = refs
    count = len(terms)
    for k, term in enumerate(terms):
        slots[lax.rem(z_ref[0] - k + count, count)] = term[...]
    total = slots[0]
    for k in range(1, count):
        total = total + slots[k]
    out_ref[...] = total * factor


def scale_kernel(factor, in_ref, out_ref):
    out_ref[...] = in_ref[...] * factor


def order_kernel(yb_ref, mine_ref, got_ref, out_ref):
    y, b = yb_ref[0], yb_ref[1]
    half = mine_ref.shape[0]
    for ref, h in ((mine_ref, y), (got_ref, 1 - y)):
        rows = pl.ds(pl.multiple_of(half * h, half), half)
        for j in range(4):
            to = pl.multiple_of(lax.bitwise_xor(b, j) * 128, 128)
            out_ref[rows, pl.ds(to, 128)] = ref[:, j * 128 : (j + 1) * 128]


def dense_kernel(yc_ref, planes_ref, proj_ref, pot_ref, e_ref, part_ref, rim_ref):
    y, c = yc_ref[0], yc_ref[1]
    e_ref[...] = jnp.zeros_like(e_ref)
    atoms, span, count, _ = proj_ref.shape
    for a in range(atoms):
        for b in range(span):
            at = (planes_ref[a, b], slice(a * count, (a + 1) * count))
            e_ref[at] = e_ref[at] + proj_ref[a, b]
    rows = pl.ds(pl.multiple_of(16 * c, 16), 16)
    for r in range(18):
        part_ref[r] = e_ref[6 * (1 - y) + r, rows, :]
    part_ref[18] = jnp.zeros(part_ref.shape[1:], F32)
    part_ref[18, : pot_ref.shape[0]] = pot_ref[...]
    rim_ref[...] = e_ref[pl.ds(18 * y, 6), rows, :]


def potential_kernel(offset, y_ref, own_ref, part_ref, out_ref):
    y = y_ref[0]
    own = own_ref[...] + offset
    other = part_ref[18, : own.shape[0]] + offset
    first, second = jnp.where(y == 0, own, other), jnp.where(y == 0, other, own)
    fill = jnp.zeros((8, own.shape[1]), F32)
    planes = jnp.concatenate([first, second, fill], axis=0)
    parts = []
    for _ in range(3):
        piece = planes.astype(BF16).astype(F32)
        parts.append(piece)
        planes = planes - piece
    out_ref[...] = jnp.concatenate(parts + [jnp.zeros_like(planes)], axis=0).T.astype(BF16)


def potential_row(pot, r):
    source = lax.broadcasted_iota(jnp.int32, (LANES, LANES), 0)
    group = lane_ids((LANES, LANES)) // QUARTER
    pick = (source % QUARTER == 6 * group + r) & (source < 3 * QUARTER)
    return lax.dot_general(
        pot, pick.astype(F32).astype(BF16), (((1,), (0,)), ((), ())), preferred_element_type=F32
    )


def gather_kernel(y_ref, part_ref, a_ref, b_ref, out_ref):
    y = y_ref[0]
    out_ref[:18] = part_ref[:18]
    for r in range(6):
        one, two = a_ref[r], b_ref[r]
        out_ref[18 + r] = jnp.where(y == 1, one, two)
        out_ref[24 + r] = jnp.where(y == 1, two, one)


def maps_kernel(yc_ref, e_ref, part_ref, part2_ref, mh_ref, ml_ref, th_ref, tl_ref):
    y, c = yc_ref[0], yc_ref[1]

    def whole(plane):
        mine, rest = part_ref[plane], part2_ref[plane]
        first, second = jnp.where(c == 0, mine, rest), jnp.where(c == 0, rest, mine)
        return jnp.concatenate([first, second], axis=0)

    for r in range(6):
        below, above = whole(18 + r), whole(24 + r)
        other = [whole(6 * i + r) for i in range(3)]
        low = [jnp.where(y == 0, e_ref[6 + 6 * i + r], other[i]) for i in range(3)]
        high = [jnp.where(y == 1, e_ref[6 * i + r], other[i]) for i in range(3)]
        block = jnp.concatenate(
            [low[0], below, low[1], high[0], low[2], high[1], above, high[2]], axis=0
        )
        mh_ref[r], ml_ref[r] = halves(block)
        th_ref[r], tl_ref[r] = halves(block.T)


SMEM = pl.BlockSpec(memory_space=pltpu.SMEM)
VMEM = pl.BlockSpec(memory_space=pltpu.VMEM)
ANY = pl.BlockSpec(memory_space=pl.ANY)


def call(kernel, out, scalars, arrays, scratch=(), after=()):
    used = len(scalars) + len(arrays)

    def body(*refs):
        kernel(*refs[:used], *refs[used + len(after) :])

    return pl.pallas_call(
        body,
        out_shape=out,
        in_specs=[SMEM] * len(scalars) + [VMEM] * len(arrays) + [ANY] * len(after),
        out_specs=[VMEM] * len(out),
        scratch_shapes=list(scratch),
        compiler_params=pltpu.CompilerParams(vmem_limit_bytes=16 * 1024 * 1024),
        cost_estimate=pl.CostEstimate(flops=1 << 10, bytes_accessed=1 << 10, transcendentals=0),
    )(*scalars, *arrays, *after)


def f32(*shape):
    return pltpu.VMEM(shape, F32)


def bf16(*shape):
    return pltpu.VMEM(shape, BF16)


def shards(orbitals, potential, projectors, atom_planes, kb_energy):
    slab, ny, nz, orb_here = orbitals.shape
    cells = ny * nz
    peers = lax.axis_size("grid")
    bands = lax.axis_size("band")
    g, b = lax.axis_index("grid"), lax.axis_index("band")
    y, c, x = lax.rem(g, 2), lax.rem(b, 2), b // 2
    y1 = y.reshape(1).astype(jnp.int32)
    z1 = (g // 2).reshape(1).astype(jnp.int32)
    yb = jnp.stack([y, b]).astype(jnp.int32)
    yc = jnp.stack([y, c]).astype(jnp.int32)
    yx = jnp.stack([y, x]).astype(jnp.int32)

    def move(array, axis, target):
        size = lax.axis_size(axis)
        return lax.ppermute(array, axis, [(i, target(i) % size) for i in range(size)])

    def partner(array):
        return move(array, "grid", lambda i: i ^ 1)

    def up(array):
        return move(array, "grid", lambda i: i + 2)

    def down(array):
        return move(array, "grid", lambda i: i - 2)

    def sibling(array):
        return move(array, "band", lambda i: i ^ 1)

    def across(array):
        return move(array, "band", lambda i: i ^ 2)

    field = orbitals.reshape(slab, cells, orb_here)
    rim_rows = 6 * (cells // 4)
    middle, scales, recall = filter_terms(DEGREE)

    def diagonal(array):
        size = peers * bands
        flip = 2 * peers + 1
        return lax.ppermute(array, ("band", "grid"), [(i, i ^ flip) for i in range(size)])

    pot_own = potential.reshape(slab, cells)
    sent0 = call(
        functools.partial(pack_kernel, 0), [f32(3 * cells, LANES)], [y1], [field]
    )[0]
    other0 = partner(sent0)
    dense, part, rim = call(
        dense_kernel,
        [f32(24, 32, cells), f32(19, 16, cells), f32(6, 16, cells)],
        [yc, atom_planes],
        [projectors.transpose(0, 2, 1, 3), pot_own],
        after=[sent0],
    )
    part = partner(part)
    rim_a = move(rim, "grid", lambda i: i + 2 if i % 2 else i - 2)
    rim_b = move(rim, "grid", lambda i: i + 1 if i % 2 else i - 1)
    sent1 = call(
        functools.partial(pack_kernel, 1),
        [f32(3 * cells, LANES)],
        [y1],
        [field],
        after=[other0],
    )[0]
    other1 = partner(sent1)
    pot_part = part
    part = call(
        gather_kernel, [f32(30, 16, cells)], [y1], [part, rim_a, rim_b], after=[sent1]
    )[0]
    mh, ml, th, tl = call(
        maps_kernel,
        [bf16(6, 256, cells)] * 2 + [bf16(6, cells, 256)] * 2,
        [yc],
        [dense, part, sibling(part)],
    )
    pot = call(
        functools.partial(potential_kernel, -(middle + 0.5 * WEIGHTS[0])),
        [bf16(cells, LANES)],
        [y1],
        [pot_own, pot_part],
        after=[mh],
    )[0]
    kb = jnp.broadcast_to(jnp.tile(kb_energy, 4)[:, None], (32, LANES))
    ch, cl = (jnp.asarray(m) for m in plane_matrix(ny, nz))

    chunks = []
    for k, got in enumerate((other0, other1)):
        made = call(
            functools.partial(assemble_kernel, k),
            [f32(6, cells, LANES)] + [f32(rim_rows + 16, LANES)] * 2 + [f32(32, LANES)],
            [y1],
            [field, got, mh, ml],
            after=[pot] if k else [],
        )
        chunks.append(
            dict(v=made[0], prev=None, below=up(made[1]), above=down(made[2]), coef=made[3])
        )

    for level in range(DEGREE):
        first, last = level == 0, level == DEGREE - 1
        for s in chunks:
            arrays = [s["v"]] + ([] if first else [s["prev"]]) + [s["below"], s["above"]]
            arrays += [s["coef"], kb, ch, cl, th, tl, pot]
            if last:
                out = [f32(rim_rows, LANES)] * 4
            else:
                arrays += [mh, ml]
                out = [f32(6, cells, LANES)] + [f32(rim_rows + 16, LANES)] * 2 + [f32(32, LANES)]
            made = call(
                functools.partial(level_kernel, scales[level], recall[level], first, last),
                out,
                [yx] if last else [],
                arrays,
                [pltpu.VMEM((18, cells, LANES), F32)],
            )
            if last:
                own, for_y, for_x, rest = made
                s["pieces"] = [own, across(for_x), partner(for_y), diagonal(rest)]
                s["for_x"], s["rest"] = for_x, rest
            else:
                s["prev"], s["v"] = s["v"], made[0]
                s["coef"], s["below"], s["above"] = made[3], up(made[1]), down(made[2])

    tile0, rest = call(
        tile_kernel,
        [f32(4 * rim_rows, LANES), f32(2 * rim_rows, LANES)],
        [y1],
        chunks[0]["pieces"] + [s["rest"] for s in chunks],
    )
    tile1 = call(tile_kernel, [f32(4 * rim_rows, LANES)], [y1], chunks[1]["pieces"])[0]
    early = call(
        gram_early_kernel, [f32(256, 384)], [], [tile0, tile1, sibling(tile0)]
    )[0]
    quarters = call(
        gram_kernel,
        [f32(64, bands * 128)] * 4,
        [y1],
        [tile0, tile1, sibling(tile1), early],
        [pltpu.VMEM((4, 64, bands * 128), F32)],
    )
    partial = call(
        add_kernel,
        [f32(64, bands * 128)],
        [],
        [quarters[0], partner(quarters[1]), across(quarters[2]), diagonal(quarters[3])],
    )[0]
    rest, partial = lax.optimization_barrier((rest, partial))
    rest = partner(rest)
    factor = 1.0 / (slab * cells * peers)
    pairs = peers // 2
    if pairs <= 4:
        moved = [partial]
        for k in range(1, pairs):
            moved.append(move(partial, "grid", lambda i, k=k: i + 2 * k))
        total = call(
            functools.partial(ring_add_kernel, factor),
            [f32(64, bands * 128)],
            [z1],
            moved,
            [pltpu.VMEM((pairs, 64, bands * 128), F32)],
            after=[rest],
        )[0]
    else:
        groups = [[2 * i + j for i in range(pairs)] for j in range(2)]
        total = lax.psum(partial, "grid", axis_index_groups=groups)
        total = call(
            functools.partial(scale_kernel, factor), [f32(64, bands * 128)], [], [total]
        )[0]
    gram = call(
        order_kernel,
        [jax.ShapeDtypeStruct((128, bands * 128), F32)],
        [yb],
        [total, partner(total)],
    )[0]
    filtered = call(
        unpack_kernel,
        [jax.ShapeDtypeStruct((slab, cells, LANES), F32)],
        [yx],
        [s["pieces"][0] for s in chunks]
        + [s["for_x"] for s in chunks]
        + [s["pieces"][2] for s in chunks]
        + [rest],
    )[0]
    return (filtered.reshape(orbitals.shape), gram)


def solution(mesh):
    return jax.shard_map(
        shards,
        mesh=mesh,
        in_specs=(
            P("grid", None, None, "band"),
            P("grid", None, None),
            P("grid", None, None, None),
            P("grid", None),
            P(),
        ),
        out_specs=(P("grid", None, None, "band"), P("band", None)),
        check_vma=False,
    )
```

```python
import functools

import jax
import jax.numpy as jnp
import ml_dtypes
import numpy as np
from jax import lax
from jax.experimental import pallas as pl
from jax.experimental.pallas import tpu as pltpu
from jax.sharding import PartitionSpec as P

DEGREE = 4
REACH = 6
LANES = 128
QUARTER = 32

WEIGHTS = (
    -5369.0 / 1800.0,
    12.0 / 7.0,
    -15.0 / 56.0,
    10.0 / 189.0,
    -1.0 / 112.0,
    2.0 / 1925.0,
    -1.0 / 16632.0,
)
LOWER = -4.0
CUTOFF = 1.0
UPPER = 16.0
F32 = jnp.float32
BF16 = jnp.bfloat16


def filter_terms(degree):
    half_span = (UPPER - CUTOFF) / 2.0
    middle = (UPPER + CUTOFF) / 2.0
    sigma_now = half_span / (LOWER - middle)
    sigma_first = sigma_now
    scales = [sigma_now / half_span]
    recall = [0.0]
    for level in range(1, degree):
        sigma_next = 1.0 / (2.0 / sigma_first - sigma_now)
        scales.append(2.0 * sigma_next / half_span)
        recall.append(sigma_now * sigma_next)
        sigma_now = sigma_next
    return (middle, scales, recall)


def plane_matrix(ny, nz):
    def ring(n):
        m = np.zeros((n, n))
        for i in range(n):
            m[i, i] += WEIGHTS[0]
            for r in range(1, REACH + 1):
                m[i, (i + r) % n] += WEIGHTS[r]
                m[i, (i - r) % n] += WEIGHTS[r]
        return m

    full = -0.5 * (np.kron(ring(ny), np.eye(nz)) + np.kron(np.eye(ny), ring(nz)))
    high = full.astype(ml_dtypes.bfloat16)
    low = (full - high.astype(np.float64)).astype(ml_dtypes.bfloat16)
    return high, low


def halves(value):
    high = value.astype(BF16)
    return high, (value - high.astype(F32)).astype(BF16)


def dot3(*pairs):
    left, right = [], []
    for (a_high, a_low), (b_high, b_low) in pairs:
        left += [a_high, a_high, a_low]
        right += [b_high, b_low, b_high]
    return lax.dot_general(
        jnp.concatenate(left, axis=1),
        jnp.concatenate(right, axis=0),
        (((1,), (0,)), ((), ())),
        preferred_element_type=F32,
    )


def lane_ids(shape):
    return lax.broadcasted_iota(jnp.int32, shape, len(shape) - 1)


def turn(value, shift):
    if isinstance(shift, int):
        shift = shift % LANES
        if shift == 0:
            return value
    else:
        shift = lax.rem(shift + 8 * LANES, LANES)
    return pltpu.roll(value, shift, axis=value.ndim - 1)


def pack_kernel(chunk, y_ref, x_ref, *refs):
    y = y_ref[0]
    out_ref = refs[-1]
    cells = x_ref.shape[1]
    group = lane_ids((cells, LANES)) // QUARTER
    if len(refs) > 1:
        out_ref[3 * cells :] = refs[0][...]
    for r in range(3):
        row = None
        for slot, plane in enumerate((r, r + 6, r + 3, r + 9)):
            piece = turn(x_ref[plane], QUARTER * slot - 64 - QUARTER * chunk + 64 * y)
            row = piece if row is None else jnp.where(group == slot, piece, row)
        out_ref[r * cells : (r + 1) * cells] = row


def rim_pack(row, out_ref, r, source):
    part = row.shape[0] // 4
    group = lane_ids((part, LANES)) // QUARTER
    packed = None
    for j in range(4):
        piece = turn(row[j * part : (j + 1) * part], QUARTER * (j - source))
        packed = piece if packed is None else jnp.where(group == j, piece, packed)
    out_ref[pl.ds(r * part, part), :] = packed


def assemble_kernel(chunk, y_ref, x_ref, got_ref, *refs):
    y = y_ref[0]
    mh_ref, ml_ref, v_ref, up_ref, down_ref, coef_ref = refs
    cells = x_ref.shape[1]
    group = lane_ids((cells, LANES)) // QUARTER
    coef = None
    for r in range(6):
        first = turn(x_ref[r], -QUARTER * chunk)
        second = turn(x_ref[r + 6], QUARTER - QUARTER * chunk)
        other = turn(
            got_ref[cells * (r % 3) : cells * (r % 3 + 1)], 64 * (1 - y) if r < 3 else 64 * y
        )
        row = jnp.where(group == 2 * y, first, jnp.where(group == 2 * y + 1, second, other))
        v_ref[r] = row
        rim_pack(row, up_ref, r, 3)
        rim_pack(row, down_ref, r, 0)
        term = dot3(((mh_ref[r], ml_ref[r]), halves(row)))
        coef = term if coef is None else coef + term
    share_coef(coef, coef_ref, up_ref, down_ref)


def share_coef(coef, coef_ref, up_ref, down_ref):
    packed = collapse(coef)
    coef_ref[...] = packed
    rim = up_ref.shape[0] - 16
    group = lane_ids((16, LANES)) // QUARTER
    top, bottom = packed[:16], packed[16:]
    up_ref[pl.ds(rim, 16), :] = jnp.where(group % 2 == 0, turn(top, -QUARTER), bottom)
    down_ref[pl.ds(rim, 16), :] = jnp.where(group % 2 == 0, top, turn(bottom, QUARTER))


def collapse(blocks):
    group = lane_ids((32, LANES)) // QUARTER

    def block(i, s, target):
        b = 2 * i + s
        return turn(blocks[32 * b : 32 * b + 32], QUARTER * (target - i))

    low = block(0, 0, 0) + block(1, 0, 0) + block(2, 0, 0)
    high = block(1, 1, 1) + block(2, 1, 1) + block(3, 1, 1)
    below, above = block(0, 1, 2), block(3, 0, 3)
    return jnp.where(
        group == 0, low, jnp.where(group == 1, high, jnp.where(group == 2, below, above))
    )


def level_kernel(scale, recall, first, last, *refs):
    refs = list(refs)
    if last:
        yx_ref = refs.pop(0)
    v_ref = refs.pop(0)
    prev_ref = None if first else refs.pop(0)
    below_ref, above_ref = refs.pop(0), refs.pop(0)
    own_ref, kb_ref, ch_ref, cl_ref, th_ref, tl_ref, pot_ref = refs[:7]
    refs = refs[7:]
    if last:
        own_piece, y_piece, x_piece, d_piece, ext = refs
    else:
        mh_ref, ml_ref, out_ref, up_ref, down_ref, coef_ref, ext = refs
    cells = v_ref.shape[1]
    part = cells // 4
    rim = 6 * part
    part_group = lane_ids((part, LANES)) // QUARTER
    cg = lane_ids((32, LANES)) // QUARTER
    low, high = below_ref[pl.ds(rim, 16), :], above_ref[pl.ds(rim, 16), :]
    from_below = jnp.concatenate([turn(low, 2 * QUARTER), turn(low, QUARTER)], axis=0)
    from_above = jnp.concatenate([turn(high, -QUARTER), turn(high, 2 * QUARTER)], axis=0)
    total = own_ref[...] + jnp.where(cg % 2 == 0, from_below, from_above)
    total = total * kb_ref[...]
    rows = []
    for i, s, source in (
        (0, 0, 0), (0, 1, 2), (1, 0, 0), (1, 1, 1), (2, 0, 0), (2, 1, 1), (3, 0, 3), (3, 1, 1),
    ):
        rows.append(jnp.where(cg == i, turn(total, QUARTER * (i - source)), 0.0))
    spread = halves(jnp.concatenate(rows, axis=0))
    for r in range(6):
        row = v_ref[r]
        ext[6 + r] = row
        before, after = turn(row, QUARTER), turn(row, -QUARTER)
        low, high = below_ref[pl.ds(r * part, part), :], above_ref[pl.ds(r * part, part), :]
        for j in range(4):
            cut = slice(j * part, (j + 1) * part)
            ext[r, cut] = jnp.where(part_group == 0, turn(low, -QUARTER * j), before[cut])
            ext[12 + r, cut] = jnp.where(part_group == 3, turn(high, 96 - QUARTER * j), after[cut])
    coef = None
    pot = pot_ref[...]
    if last:
        mine = 2 * yx_ref[0] + yx_ref[1]
    for r in range(6):
        row = ext[6 + r]
        value = dot3(
            ((ch_ref[...], cl_ref[...]), halves(row)), ((th_ref[r], tl_ref[r]), spread)
        )
        value = value + potential_row(pot, r) * row
        for k in range(1, REACH + 1):
            value = value + (-0.5 * WEIGHTS[k]) * (ext[6 + r + k] + ext[6 + r - k])
        value = scale * value
        if not first:
            value = value - recall * prev_ref[r]
        if last:
            for flip, piece in enumerate((own_piece, x_piece, y_piece, d_piece)):
                rim_pack(value, piece, r, lax.bitwise_xor(mine, flip))
        else:
            out_ref[r] = value
            rim_pack(value, up_ref, r, 3)
            rim_pack(value, down_ref, r, 0)
            term = dot3(((mh_ref[r], ml_ref[r]), halves(value)))
            coef = term if coef is None else coef + term
    if not last:
        share_coef(coef, coef_ref, up_ref, down_ref)


def unpack_kernel(
    yx_ref, own0_ref, own1_ref, x0_ref, x1_ref, y0_ref, y1_ref, rest_ref, out_ref
):
    y, x = yx_ref[0], yx_ref[1]
    cells = out_ref.shape[1]
    part = cells // 4
    rim = 6 * part
    group = lane_ids((part, LANES)) // QUARTER
    rest = [rest_ref.at[pl.ds(k * rim, rim)] for k in range(2)]
    for half, own, got in (
        (x, (own0_ref, own1_ref), (y0_ref, y1_ref)),
        (1 - x, (x0_ref, x1_ref), rest),
    ):
        for r in range(6):
            for j in range(4):
                block = None
                for k in range(2):
                    here = turn(own[k][pl.ds(r * part, part), :], 64 * y + QUARTER * (k - j))
                    there = turn(got[k][pl.ds(r * part, part), :], 64 * (1 - y) + QUARTER * (k - j))
                    mine = jnp.where(group == 2 * y + k, here, there)
                    block = mine if k == 0 else jnp.where(group % 2 == 1, mine, block)
                out_ref[6 * half + r, j * part : (j + 1) * part] = block


def tile_kernel(y_ref, own_ref, x_ref, y_piece_ref, d_ref, *refs):
    y = y_ref[0]
    rows = own_ref.shape[0]
    out_ref = refs[2] if len(refs) > 2 else refs[0]
    if len(refs) > 2:
        refs[3][:rows] = refs[0][...]
        refs[3][rows:] = refs[1][...]
    pieces = [own_ref[...], y_piece_ref[...], x_ref[...], d_ref[...]]
    group = lane_ids((rows, LANES)) // QUARTER
    for j in range(4):
        block = None
        for s, piece in enumerate(pieces):
            target = 2 * (s // 2) + lax.bitwise_xor(y, s % 2)
            turned = turn(piece, QUARTER * (target - j))
            block = turned if block is None else jnp.where(group == target, turned, block)
        out_ref[pl.ds(j * rows, rows), :] = block


def gram_product(left, right):
    def dot(p, q):
        return lax.dot_general(p, q, (((0,), (0,)), ((), ())), preferred_element_type=F32)

    def side(parts, i):
        return jnp.concatenate([p[i] for p in parts], axis=1)

    high, low = side(left, 0), side(left, 1)
    return dot(high, side(right, 0)) + (dot(high, side(right, 1)) + dot(low, side(right, 0)))


def gram_early_kernel(a0_ref, a1_ref, s0_ref, out_ref):
    parts = [halves(ref[...]) for ref in (a0_ref, a1_ref, s0_ref)]
    out_ref[...] = gram_product(parts[:2], parts)


def gram_kernel(
    y_ref, a0_ref, a1_ref, s1_ref, early_ref, own_ref, to_y_ref, to_x_ref, to_d_ref, parts_ref
):
    parts = [halves(ref[...]) for ref in (a0_ref, a1_ref, s1_ref)]
    late = gram_product(parts[:2], parts[2:])
    total = jnp.concatenate([early_ref[...], late], axis=1)
    group = lane_ids((32, LANES)) // QUARTER
    for x_row in range(2):
        for h_row in range(2):
            for k_row in range(2):
                at = 128 * k_row + 64 * x_row + 32 * h_row
                for flip in range(4):
                    x_col, core = flip // 2, flip % 2
                    block = None
                    for h in range(2):
                        for k in range(2):
                            start = 256 * core + 128 * k
                            tile = total[at : at + 32, start : start + 128]
                            piece = turn(tile, QUARTER * (2 * h + k - 2 * x_col - h))
                            block = (
                                piece
                                if block is None
                                else jnp.where(group == 2 * h + k, piece, block)
                            )
                    to = 2 * (x_col ^ x_row) + core
                    rows = slice(32 * k_row, 32 * k_row + 32)
                    parts_ref[2 * x_row + h_row, rows, 128 * to : 128 * to + 128] = block
    y = y_ref[0]
    own_ref[...] = parts_ref[y]
    to_y_ref[...] = parts_ref[1 - y]
    to_x_ref[...] = parts_ref[2 + y]
    to_d_ref[...] = parts_ref[3 - y]


def add_kernel(*refs):
    *terms, out_ref = refs
    out_ref[...] = (terms[0][...] + terms[1][...]) + (terms[2][...] + terms[3][...])


def ring_add_kernel(factor, z_ref, *refs):
    *terms, out_ref, slots = refs
    count = len(terms)
    for k, term in enumerate(terms):
        slots[lax.rem(z_ref[0] - k + count, count)] = term[...]
    total = slots[0]
    for k in range(1, count):
        total = total + slots[k]
    out_ref[...] = total * factor


def scale_kernel(factor, in_ref, out_ref):
    out_ref[...] = in_ref[...] * factor


def order_kernel(yb_ref, mine_ref, got_ref, out_ref):
    y, b = yb_ref[0], yb_ref[1]
    half = mine_ref.shape[0]
    for ref, h in ((mine_ref, y), (got_ref, 1 - y)):
        rows = pl.ds(pl.multiple_of(half * h, half), half)
        for j in range(4):
            to = pl.multiple_of(lax.bitwise_xor(b, j) * 128, 128)
            out_ref[rows, pl.ds(to, 128)] = ref[:, j * 128 : (j + 1) * 128]


def dense_kernel(yc_ref, planes_ref, proj_ref, pot_ref, e_ref, part_ref, rim_ref):
    y, c = yc_ref[0], yc_ref[1]
    e_ref[...] = jnp.zeros_like(e_ref)
    atoms, span, count, _ = proj_ref.shape
    for a in range(atoms):
        for b in range(span):
            at = (planes_ref[a, b], slice(a * count, (a + 1) * count))
            e_ref[at] = e_ref[at] + proj_ref[a, b]
    rows = pl.ds(pl.multiple_of(16 * c, 16), 16)
    for r in range(18):
        part_ref[r] = e_ref[6 * (1 - y) + r, rows, :]
    part_ref[18] = jnp.zeros(part_ref.shape[1:], F32)
    part_ref[18, : pot_ref.shape[0]] = pot_ref[...]
    rim_ref[...] = e_ref[pl.ds(18 * y, 6), rows, :]


def potential_kernel(offset, y_ref, own_ref, part_ref, out_ref):
    y = y_ref[0]
    own = own_ref[...] + offset
    other = part_ref[18, : own.shape[0]] + offset
    first, second = jnp.where(y == 0, own, other), jnp.where(y == 0, other, own)
    fill = jnp.zeros((8, own.shape[1]), F32)
    planes = jnp.concatenate([first, second, fill], axis=0)
    parts = []
    for _ in range(3):
        piece = planes.astype(BF16).astype(F32)
        parts.append(piece)
        planes = planes - piece
    out_ref[...] = jnp.concatenate(parts + [jnp.zeros_like(planes)], axis=0).T.astype(BF16)


def potential_row(pot, r):
    source = lax.broadcasted_iota(jnp.int32, (LANES, LANES), 0)
    group = lane_ids((LANES, LANES)) // QUARTER
    pick = (source % QUARTER == 6 * group + r) & (source < 3 * QUARTER)
    return lax.dot_general(
        pot, pick.astype(F32).astype(BF16), (((1,), (0,)), ((), ())), preferred_element_type=F32
    )


def gather_kernel(y_ref, part_ref, a_ref, b_ref, out_ref):
    y = y_ref[0]
    out_ref[:18] = part_ref[:18]
    for r in range(6):
        one, two = a_ref[r], b_ref[r]
        out_ref[18 + r] = jnp.where(y == 1, one, two)
        out_ref[24 + r] = jnp.where(y == 1, two, one)


def maps_kernel(yc_ref, e_ref, part_ref, part2_ref, mh_ref, ml_ref, th_ref, tl_ref):
    y, c = yc_ref[0], yc_ref[1]

    def whole(plane):
        mine, rest = part_ref[plane], part2_ref[plane]
        first, second = jnp.where(c == 0, mine, rest), jnp.where(c == 0, rest, mine)
        return jnp.concatenate([first, second], axis=0)

    for r in range(6):
        below, above = whole(18 + r), whole(24 + r)
        other = [whole(6 * i + r) for i in range(3)]
        low = [jnp.where(y == 0, e_ref[6 + 6 * i + r], other[i]) for i in range(3)]
        high = [jnp.where(y == 1, e_ref[6 * i + r], other[i]) for i in range(3)]
        block = jnp.concatenate(
            [low[0], below, low[1], high[0], low[2], high[1], above, high[2]], axis=0
        )
        mh_ref[r], ml_ref[r] = halves(block)
        th_ref[r], tl_ref[r] = halves(block.T)


SMEM = pl.BlockSpec(memory_space=pltpu.SMEM)
VMEM = pl.BlockSpec(memory_space=pltpu.VMEM)
ANY = pl.BlockSpec(memory_space=pl.ANY)


def call(kernel, out, scalars, arrays, scratch=(), after=(), cost=1 << 10):
    used = len(scalars) + len(arrays)

    def body(*refs):
        kernel(*refs[:used], *refs[used + len(after) :])

    return pl.pallas_call(
        body,
        out_shape=out,
        in_specs=[SMEM] * len(scalars) + [VMEM] * len(arrays) + [ANY] * len(after),
        out_specs=[VMEM] * len(out),
        scratch_shapes=list(scratch),
        compiler_params=pltpu.CompilerParams(vmem_limit_bytes=16 * 1024 * 1024),
        cost_estimate=pl.CostEstimate(flops=cost, bytes_accessed=1 << 10, transcendentals=0),
    )(*scalars, *arrays, *after)


def f32(*shape):
    return pltpu.VMEM(shape, F32)


def bf16(*shape):
    return pltpu.VMEM(shape, BF16)


def shards(orbitals, potential, projectors, atom_planes, kb_energy):
    slab, ny, nz, orb_here = orbitals.shape
    cells = ny * nz
    peers = lax.axis_size("grid")
    bands = lax.axis_size("band")
    g, b = lax.axis_index("grid"), lax.axis_index("band")
    y, c, x = lax.rem(g, 2), lax.rem(b, 2), b // 2
    y1 = y.reshape(1).astype(jnp.int32)
    z1 = (g // 2).reshape(1).astype(jnp.int32)
    yb = jnp.stack([y, b]).astype(jnp.int32)
    yc = jnp.stack([y, c]).astype(jnp.int32)
    yx = jnp.stack([y, x]).astype(jnp.int32)

    def move(array, axis, target):
        size = lax.axis_size(axis)
        return lax.ppermute(array, axis, [(i, target(i) % size) for i in range(size)])

    def partner(array):
        return move(array, "grid", lambda i: i ^ 1)

    def up(array):
        return move(array, "grid", lambda i: i + 2)

    def down(array):
        return move(array, "grid", lambda i: i - 2)

    def sibling(array):
        return move(array, "band", lambda i: i ^ 1)

    def across(array):
        return move(array, "band", lambda i: i ^ 2)

    field = orbitals.reshape(slab, cells, orb_here)
    rim_rows = 6 * (cells // 4)
    middle, scales, recall = filter_terms(DEGREE)

    def diagonal(array):
        size = peers * bands
        flip = 2 * peers + 1
        return lax.ppermute(array, ("band", "grid"), [(i, i ^ flip) for i in range(size)])

    pot_own = potential.reshape(slab, cells)
    sent0 = call(
        functools.partial(pack_kernel, 0), [f32(3 * cells, LANES)], [y1], [field]
    )[0]
    other0 = partner(sent0)
    dense, part, rim = call(
        dense_kernel,
        [f32(24, 32, cells), f32(19, 16, cells), f32(6, 16, cells)],
        [yc, atom_planes],
        [projectors.transpose(0, 2, 1, 3), pot_own],
        after=[sent0],
    )
    part = partner(part)
    rim_a = move(rim, "grid", lambda i: i + 2 if i % 2 else i - 2)
    rim_b = move(rim, "grid", lambda i: i + 1 if i % 2 else i - 1)
    sent1 = call(
        functools.partial(pack_kernel, 1),
        [f32(3 * cells, LANES)],
        [y1],
        [field],
        after=[other0],
    )[0]
    other1 = partner(sent1)
    pot_part = part
    part = call(
        gather_kernel, [f32(30, 16, cells)], [y1], [part, rim_a, rim_b], after=[sent1]
    )[0]
    mh, ml, th, tl = call(
        maps_kernel,
        [bf16(6, 256, cells)] * 2 + [bf16(6, cells, 256)] * 2,
        [yc],
        [dense, part, sibling(part)],
    )
    pot = call(
        functools.partial(potential_kernel, -(middle + 0.5 * WEIGHTS[0])),
        [bf16(cells, LANES)],
        [y1],
        [pot_own, pot_part],
        after=[mh],
    )[0]
    kb = jnp.broadcast_to(jnp.tile(kb_energy, 4)[:, None], (32, LANES))
    ch, cl = (jnp.asarray(m) for m in plane_matrix(ny, nz))

    chunks = []
    for k, got in enumerate((other0, other1)):
        made = call(
            functools.partial(assemble_kernel, k),
            [f32(6, cells, LANES)] + [f32(rim_rows + 16, LANES)] * 2 + [f32(32, LANES)],
            [y1],
            [field, got, mh, ml],
            after=[pot] if k else [],
        )
        chunks.append(
            dict(v=made[0], prev=None, below=up(made[1]), above=down(made[2]), coef=made[3])
        )

    for level in range(DEGREE):
        first, last = level == 0, level == DEGREE - 1
        for s in chunks:
            arrays = [s["v"]] + ([] if first else [s["prev"]]) + [s["below"], s["above"]]
            arrays += [s["coef"], kb, ch, cl, th, tl, pot]
            if last:
                out = [f32(rim_rows, LANES)] * 4
            else:
                arrays += [mh, ml]
                out = [f32(6, cells, LANES)] + [f32(rim_rows + 16, LANES)] * 2 + [f32(32, LANES)]
            made = call(
                functools.partial(level_kernel, scales[level], recall[level], first, last),
                out,
                [yx] if last else [],
                arrays,
                [pltpu.VMEM((18, cells, LANES), F32)],
                cost=1 << 30,
            )
            if last:
                own, for_y, for_x, rest = made
                s["pieces"] = [own, across(for_x), partner(for_y), diagonal(rest)]
                s["for_x"], s["rest"] = for_x, rest
            else:
                s["prev"], s["v"] = s["v"], made[0]
                s["coef"], s["below"], s["above"] = made[3], up(made[1]), down(made[2])

    tile0, rest = call(
        tile_kernel,
        [f32(4 * rim_rows, LANES), f32(2 * rim_rows, LANES)],
        [y1],
        chunks[0]["pieces"] + [s["rest"] for s in chunks],
    )
    tile1 = call(tile_kernel, [f32(4 * rim_rows, LANES)], [y1], chunks[1]["pieces"])[0]
    early = call(
        gram_early_kernel, [f32(256, 384)], [], [tile0, tile1, sibling(tile0)]
    )[0]
    quarters = call(
        gram_kernel,
        [f32(64, bands * 128)] * 4,
        [y1],
        [tile0, tile1, sibling(tile1), early],
        [pltpu.VMEM((4, 64, bands * 128), F32)],
    )
    partial = call(
        add_kernel,
        [f32(64, bands * 128)],
        [],
        [quarters[0], partner(quarters[1]), across(quarters[2]), diagonal(quarters[3])],
    )[0]
    rest, partial = lax.optimization_barrier((rest, partial))
    rest = partner(rest)
    factor = 1.0 / (slab * cells * peers)
    pairs = peers // 2
    if pairs <= 4:
        moved = [partial]
        for k in range(1, pairs):
            moved.append(move(partial, "grid", lambda i, k=k: i + 2 * k))
        total = call(
            functools.partial(ring_add_kernel, factor),
            [f32(64, bands * 128)],
            [z1],
            moved,
            [pltpu.VMEM((pairs, 64, bands * 128), F32)],
            after=[rest],
        )[0]
    else:
        groups = [[2 * i + j for i in range(pairs)] for j in range(2)]
        total = lax.psum(partial, "grid", axis_index_groups=groups)
        total = call(
            functools.partial(scale_kernel, factor), [f32(64, bands * 128)], [], [total]
        )[0]
    gram = call(
        order_kernel,
        [jax.ShapeDtypeStruct((128, bands * 128), F32)],
        [yb],
        [total, partner(total)],
    )[0]
    filtered = call(
        unpack_kernel,
        [jax.ShapeDtypeStruct((slab, cells, LANES), F32)],
        [yx],
        [s["pieces"][0] for s in chunks]
        + [s["for_x"] for s in chunks]
        + [s["pieces"][2] for s in chunks]
        + [rest],
    )[0]
    return (filtered.reshape(orbitals.shape), gram)


def solution(mesh):
    return jax.shard_map(
        shards,
        mesh=mesh,
        in_specs=(
            P("grid", None, None, "band"),
            P("grid", None, None),
            P("grid", None, None, None),
            P("grid", None),
            P(),
        ),
        out_specs=(P("grid", None, None, "band"), P("band", None)),
        check_vma=False,
    )
```

```python
import functools

import jax
import jax.numpy as jnp
import ml_dtypes
import numpy as np
from jax import lax
from jax.experimental import pallas as pl
from jax.experimental.pallas import tpu as pltpu
from jax.sharding import PartitionSpec as P

DEGREE = 4
REACH = 6
LANES = 128
QUARTER = 32

WEIGHTS = (
    -5369.0 / 1800.0,
    12.0 / 7.0,
    -15.0 / 56.0,
    10.0 / 189.0,
    -1.0 / 112.0,
    2.0 / 1925.0,
    -1.0 / 16632.0,
)
LOWER = -4.0
CUTOFF = 1.0
UPPER = 16.0
F32 = jnp.float32
BF16 = jnp.bfloat16


def filter_terms(degree):
    half_span = (UPPER - CUTOFF) / 2.0
    middle = (UPPER + CUTOFF) / 2.0
    sigma_now = half_span / (LOWER - middle)
    sigma_first = sigma_now
    scales = [sigma_now / half_span]
    recall = [0.0]
    for level in range(1, degree):
        sigma_next = 1.0 / (2.0 / sigma_first - sigma_now)
        scales.append(2.0 * sigma_next / half_span)
        recall.append(sigma_now * sigma_next)
        sigma_now = sigma_next
    return (middle, scales, recall)


def plane_matrix(ny, nz):
    def ring(n):
        m = np.zeros((n, n))
        for i in range(n):
            m[i, i] += WEIGHTS[0]
            for r in range(1, REACH + 1):
                m[i, (i + r) % n] += WEIGHTS[r]
                m[i, (i - r) % n] += WEIGHTS[r]
        return m

    full = -0.5 * (np.kron(ring(ny), np.eye(nz)) + np.kron(np.eye(ny), ring(nz)))
    high = full.astype(ml_dtypes.bfloat16)
    low = (full - high.astype(np.float64)).astype(ml_dtypes.bfloat16)
    return high, low


def halves(value):
    high = value.astype(BF16)
    return high, (value - high.astype(F32)).astype(BF16)


def dot3(*pairs):
    left, right = [], []
    for (a_high, a_low), (b_high, b_low) in pairs:
        left += [a_high, a_high, a_low]
        right += [b_high, b_low, b_high]
    return lax.dot_general(
        jnp.concatenate(left, axis=1),
        jnp.concatenate(right, axis=0),
        (((1,), (0,)), ((), ())),
        preferred_element_type=F32,
    )


def lane_ids(shape):
    return lax.broadcasted_iota(jnp.int32, shape, len(shape) - 1)


def turn(value, shift):
    if isinstance(shift, int):
        shift = shift % LANES
        if shift == 0:
            return value
    else:
        shift = lax.rem(shift + 8 * LANES, LANES)
    return pltpu.roll(value, shift, axis=value.ndim - 1)


def pack_kernel(chunk, y_ref, x_ref, *refs):
    y = y_ref[0]
    out_ref = refs[-1]
    cells = x_ref.shape[1]
    group = lane_ids((cells, LANES)) // QUARTER
    if len(refs) > 1:
        out_ref[3 * cells :] = refs[0][...]
    for r in range(3):
        row = None
        for slot, plane in enumerate((r, r + 6, r + 3, r + 9)):
            piece = turn(x_ref[plane], QUARTER * slot - 64 - QUARTER * chunk + 64 * y)
            row = piece if row is None else jnp.where(group == slot, piece, row)
        out_ref[r * cells : (r + 1) * cells] = row


def rim_pack(row, out_ref, r, source):
    part = row.shape[0] // 4
    group = lane_ids((part, LANES)) // QUARTER
    packed = None
    for j in range(4):
        piece = turn(row[j * part : (j + 1) * part], QUARTER * (j - source))
        packed = piece if packed is None else jnp.where(group == j, piece, packed)
    out_ref[pl.ds(r * part, part), :] = packed


def assemble_kernel(chunk, y_ref, x_ref, got_ref, *refs):
    y = y_ref[0]
    mh_ref, ml_ref, v_ref, up_ref, down_ref, coef_ref = refs
    cells = x_ref.shape[1]
    group = lane_ids((cells, LANES)) // QUARTER
    coef = None
    for r in range(6):
        first = turn(x_ref[r], -QUARTER * chunk)
        second = turn(x_ref[r + 6], QUARTER - QUARTER * chunk)
        other = turn(
            got_ref[cells * (r % 3) : cells * (r % 3 + 1)], 64 * (1 - y) if r < 3 else 64 * y
        )
        row = jnp.where(group == 2 * y, first, jnp.where(group == 2 * y + 1, second, other))
        v_ref[r] = row
        rim_pack(row, up_ref, r, 3)
        rim_pack(row, down_ref, r, 0)
        term = dot3(((mh_ref[r], ml_ref[r]), halves(row)))
        coef = term if coef is None else coef + term
    share_coef(coef, coef_ref, up_ref, down_ref)


def share_coef(coef, coef_ref, up_ref, down_ref):
    packed = collapse(coef)
    coef_ref[...] = packed
    rim = up_ref.shape[0] - 16
    group = lane_ids((16, LANES)) // QUARTER
    top, bottom = packed[:16], packed[16:]
    up_ref[pl.ds(rim, 16), :] = jnp.where(group % 2 == 0, turn(top, -QUARTER), bottom)
    down_ref[pl.ds(rim, 16), :] = jnp.where(group % 2 == 0, top, turn(bottom, QUARTER))


def collapse(blocks):
    group = lane_ids((32, LANES)) // QUARTER

    def block(i, s, target):
        b = 2 * i + s
        return turn(blocks[32 * b : 32 * b + 32], QUARTER * (target - i))

    low = block(0, 0, 0) + block(1, 0, 0) + block(2, 0, 0)
    high = block(1, 1, 1) + block(2, 1, 1) + block(3, 1, 1)
    below, above = block(0, 1, 2), block(3, 0, 3)
    return jnp.where(
        group == 0, low, jnp.where(group == 1, high, jnp.where(group == 2, below, above))
    )


def level_kernel(scale, recall, first, last, *refs):
    refs = list(refs)
    if last:
        yx_ref = refs.pop(0)
    v_ref = refs.pop(0)
    prev_ref = None if first else refs.pop(0)
    below_ref, above_ref = refs.pop(0), refs.pop(0)
    own_ref, kb_ref, ch_ref, cl_ref, th_ref, tl_ref, pot_ref = refs[:7]
    refs = refs[7:]
    if last:
        own_piece, y_piece, x_piece, d_piece, ext = refs
    else:
        mh_ref, ml_ref, out_ref, up_ref, down_ref, coef_ref, ext = refs
    cells = v_ref.shape[1]
    part = cells // 4
    rim = 6 * part
    part_group = lane_ids((part, LANES)) // QUARTER
    cg = lane_ids((32, LANES)) // QUARTER
    low, high = below_ref[pl.ds(rim, 16), :], above_ref[pl.ds(rim, 16), :]
    from_below = jnp.concatenate([turn(low, 2 * QUARTER), turn(low, QUARTER)], axis=0)
    from_above = jnp.concatenate([turn(high, -QUARTER), turn(high, 2 * QUARTER)], axis=0)
    total = own_ref[...] + jnp.where(cg % 2 == 0, from_below, from_above)
    total = total * kb_ref[...]
    rows = []
    for i, s, source in (
        (0, 0, 0), (0, 1, 2), (1, 0, 0), (1, 1, 1), (2, 0, 0), (2, 1, 1), (3, 0, 3), (3, 1, 1),
    ):
        rows.append(jnp.where(cg == i, turn(total, QUARTER * (i - source)), 0.0))
    spread = halves(jnp.concatenate(rows, axis=0))
    for r in range(6):
        row = v_ref[r]
        ext[6 + r] = row
        before, after = turn(row, QUARTER), turn(row, -QUARTER)
        low, high = below_ref[pl.ds(r * part, part), :], above_ref[pl.ds(r * part, part), :]
        for j in range(4):
            cut = slice(j * part, (j + 1) * part)
            ext[r, cut] = jnp.where(part_group == 0, turn(low, -QUARTER * j), before[cut])
            ext[12 + r, cut] = jnp.where(part_group == 3, turn(high, 96 - QUARTER * j), after[cut])
    coef = None
    pot = pot_ref[...]
    if last:
        mine = 2 * yx_ref[0] + yx_ref[1]
    for r in range(6):
        row = ext[6 + r]
        value = dot3(
            ((ch_ref[...], cl_ref[...]), halves(row)), ((th_ref[r], tl_ref[r]), spread)
        )
        value = value + potential_row(pot, r) * row
        for k in range(1, REACH + 1):
            value = value + (-0.5 * WEIGHTS[k]) * (ext[6 + r + k] + ext[6 + r - k])
        value = scale * value
        if not first:
            value = value - recall * prev_ref[r]
        if last:
            for flip, piece in enumerate((own_piece, x_piece, y_piece, d_piece)):
                rim_pack(value, piece, r, lax.bitwise_xor(mine, flip))
        else:
            out_ref[r] = value
            rim_pack(value, up_ref, r, 3)
            rim_pack(value, down_ref, r, 0)
            term = dot3(((mh_ref[r], ml_ref[r]), halves(value)))
            coef = term if coef is None else coef + term
    if not last:
        share_coef(coef, coef_ref, up_ref, down_ref)


def unpack_kernel(
    yx_ref, own0_ref, own1_ref, x0_ref, x1_ref, y0_ref, y1_ref, rest_ref, out_ref
):
    y, x = yx_ref[0], yx_ref[1]
    cells = out_ref.shape[1]
    part = cells // 4
    rim = 6 * part
    group = lane_ids((part, LANES)) // QUARTER
    rest = [rest_ref.at[pl.ds(k * rim, rim)] for k in range(2)]
    for half, own, got in (
        (x, (own0_ref, own1_ref), (y0_ref, y1_ref)),
        (1 - x, (x0_ref, x1_ref), rest),
    ):
        for r in range(6):
            for j in range(4):
                block = None
                for k in range(2):
                    here = turn(own[k][pl.ds(r * part, part), :], 64 * y + QUARTER * (k - j))
                    there = turn(got[k][pl.ds(r * part, part), :], 64 * (1 - y) + QUARTER * (k - j))
                    mine = jnp.where(group == 2 * y + k, here, there)
                    block = mine if k == 0 else jnp.where(group % 2 == 1, mine, block)
                out_ref[6 * half + r, j * part : (j + 1) * part] = block


def tile_kernel(y_ref, own_ref, x_ref, y_piece_ref, d_ref, *refs):
    y = y_ref[0]
    rows = own_ref.shape[0]
    out_ref = refs[2] if len(refs) > 2 else refs[0]
    if len(refs) > 2:
        refs[3][:rows] = refs[0][...]
        refs[3][rows:] = refs[1][...]
    pieces = [own_ref[...], y_piece_ref[...], x_ref[...], d_ref[...]]
    group = lane_ids((rows, LANES)) // QUARTER
    for j in range(4):
        block = None
        for s, piece in enumerate(pieces):
            target = 2 * (s // 2) + lax.bitwise_xor(y, s % 2)
            turned = turn(piece, QUARTER * (target - j))
            block = turned if block is None else jnp.where(group == target, turned, block)
        out_ref[pl.ds(j * rows, rows), :] = block


def gram_product(left, right):
    def dot(p, q):
        return lax.dot_general(p, q, (((0,), (0,)), ((), ())), preferred_element_type=F32)

    def side(parts, i):
        return jnp.concatenate([p[i] for p in parts], axis=1)

    high, low = side(left, 0), side(left, 1)
    return dot(high, side(right, 0)) + (dot(high, side(right, 1)) + dot(low, side(right, 0)))


def gram_early_kernel(a0_ref, a1_ref, s0_ref, out_ref):
    parts = [halves(ref[...]) for ref in (a0_ref, a1_ref, s0_ref)]
    out_ref[...] = gram_product(parts[:2], parts)


def gram_kernel(
    y_ref, a0_ref, a1_ref, s1_ref, early_ref, own_ref, to_y_ref, to_x_ref, to_d_ref, parts_ref
):
    parts = [halves(ref[...]) for ref in (a0_ref, a1_ref, s1_ref)]
    late = gram_product(parts[:2], parts[2:])
    total = jnp.concatenate([early_ref[...], late], axis=1)
    group = lane_ids((32, LANES)) // QUARTER
    for x_row in range(2):
        for h_row in range(2):
            for k_row in range(2):
                at = 128 * k_row + 64 * x_row + 32 * h_row
                for flip in range(4):
                    x_col, core = flip // 2, flip % 2
                    block = None
                    for h in range(2):
                        for k in range(2):
                            start = 256 * core + 128 * k
                            tile = total[at : at + 32, start : start + 128]
                            piece = turn(tile, QUARTER * (2 * h + k - 2 * x_col - h))
                            block = (
                                piece
                                if block is None
                                else jnp.where(group == 2 * h + k, piece, block)
                            )
                    to = 2 * (x_col ^ x_row) + core
                    rows = slice(32 * k_row, 32 * k_row + 32)
                    parts_ref[2 * x_row + h_row, rows, 128 * to : 128 * to + 128] = block
    y = y_ref[0]
    own_ref[...] = parts_ref[y]
    to_y_ref[...] = parts_ref[1 - y]
    to_x_ref[...] = parts_ref[2 + y]
    to_d_ref[...] = parts_ref[3 - y]


def add_kernel(*refs):
    *terms, out_ref = refs
    out_ref[...] = (terms[0][...] + terms[1][...]) + (terms[2][...] + terms[3][...])


def ring_add_kernel(factor, z_ref, *refs):
    *terms, out_ref, slots = refs
    count = len(terms)
    for k, term in enumerate(terms):
        slots[lax.rem(z_ref[0] - k + count, count)] = term[...]
    total = slots[0]
    for k in range(1, count):
        total = total + slots[k]
    out_ref[...] = total * factor


def scale_kernel(factor, in_ref, out_ref):
    out_ref[...] = in_ref[...] * factor


def order_kernel(yb_ref, mine_ref, got_ref, out_ref):
    y, b = yb_ref[0], yb_ref[1]
    half = mine_ref.shape[0]
    for ref, h in ((mine_ref, y), (got_ref, 1 - y)):
        rows = pl.ds(pl.multiple_of(half * h, half), half)
        for j in range(4):
            to = pl.multiple_of(lax.bitwise_xor(b, j) * 128, 128)
            out_ref[rows, pl.ds(to, 128)] = ref[:, j * 128 : (j + 1) * 128]


def dense_kernel(yc_ref, planes_ref, proj_ref, pot_ref, e_ref, part_ref, rim_ref):
    y, c = yc_ref[0], yc_ref[1]
    e_ref[...] = jnp.zeros_like(e_ref)
    atoms, span, count, _ = proj_ref.shape
    for a in range(atoms):
        for b in range(span):
            at = (planes_ref[a, b], slice(a * count, (a + 1) * count))
            e_ref[at] = e_ref[at] + proj_ref[a, b]
    rows = pl.ds(pl.multiple_of(16 * c, 16), 16)
    for r in range(18):
        part_ref[r] = e_ref[6 * (1 - y) + r, rows, :]
    part_ref[18] = jnp.zeros(part_ref.shape[1:], F32)
    part_ref[18, : pot_ref.shape[0]] = pot_ref[...]
    rim_ref[...] = e_ref[pl.ds(18 * y, 6), rows, :]


def potential_kernel(offset, y_ref, own_ref, part_ref, out_ref):
    y = y_ref[0]
    own = own_ref[...] + offset
    other = part_ref[18, : own.shape[0]] + offset
    first, second = jnp.where(y == 0, own, other), jnp.where(y == 0, other, own)
    fill = jnp.zeros((8, own.shape[1]), F32)
    planes = jnp.concatenate([first, second, fill], axis=0)
    parts = []
    for _ in range(3):
        piece = planes.astype(BF16).astype(F32)
        parts.append(piece)
        planes = planes - piece
    out_ref[...] = jnp.concatenate(parts + [jnp.zeros_like(planes)], axis=0).T.astype(BF16)


def potential_row(pot, r):
    source = lax.broadcasted_iota(jnp.int32, (LANES, LANES), 0)
    group = lane_ids((LANES, LANES)) // QUARTER
    pick = (source % QUARTER == 6 * group + r) & (source < 3 * QUARTER)
    return lax.dot_general(
        pot, pick.astype(F32).astype(BF16), (((1,), (0,)), ((), ())), preferred_element_type=F32
    )


def gather_kernel(y_ref, part_ref, a_ref, b_ref, out_ref):
    y = y_ref[0]
    out_ref[:18] = part_ref[:18]
    for r in range(6):
        one, two = a_ref[r], b_ref[r]
        out_ref[18 + r] = jnp.where(y == 1, one, two)
        out_ref[24 + r] = jnp.where(y == 1, two, one)


def maps_kernel(yc_ref, e_ref, part_ref, part2_ref, mh_ref, ml_ref, th_ref, tl_ref):
    y, c = yc_ref[0], yc_ref[1]

    def whole(plane):
        mine, rest = part_ref[plane], part2_ref[plane]
        first, second = jnp.where(c == 0, mine, rest), jnp.where(c == 0, rest, mine)
        return jnp.concatenate([first, second], axis=0)

    for r in range(6):
        below, above = whole(18 + r), whole(24 + r)
        other = [whole(6 * i + r) for i in range(3)]
        low = [jnp.where(y == 0, e_ref[6 + 6 * i + r], other[i]) for i in range(3)]
        high = [jnp.where(y == 1, e_ref[6 * i + r], other[i]) for i in range(3)]
        block = jnp.concatenate(
            [low[0], below, low[1], high[0], low[2], high[1], above, high[2]], axis=0
        )
        mh_ref[r], ml_ref[r] = halves(block)
        th_ref[r], tl_ref[r] = halves(block.T)


SMEM = pl.BlockSpec(memory_space=pltpu.SMEM)
VMEM = pl.BlockSpec(memory_space=pltpu.VMEM)
ANY = pl.BlockSpec(memory_space=pl.ANY)


def call(kernel, out, scalars, arrays, scratch=(), after=(), cost=1 << 10):
    used = len(scalars) + len(arrays)

    def body(*refs):
        kernel(*refs[:used], *refs[used + len(after) :])

    return pl.pallas_call(
        body,
        out_shape=out,
        in_specs=[SMEM] * len(scalars) + [VMEM] * len(arrays) + [ANY] * len(after),
        out_specs=[VMEM] * len(out),
        scratch_shapes=list(scratch),
        compiler_params=pltpu.CompilerParams(vmem_limit_bytes=16 * 1024 * 1024),
        cost_estimate=pl.CostEstimate(flops=cost, bytes_accessed=1 << 10, transcendentals=0),
    )(*scalars, *arrays, *after)


def f32(*shape):
    return pltpu.VMEM(shape, F32)


def bf16(*shape):
    return pltpu.VMEM(shape, BF16)


def shards(orbitals, potential, projectors, atom_planes, kb_energy):
    slab, ny, nz, orb_here = orbitals.shape
    cells = ny * nz
    peers = lax.axis_size("grid")
    bands = lax.axis_size("band")
    g, b = lax.axis_index("grid"), lax.axis_index("band")
    y, c, x = lax.rem(g, 2), lax.rem(b, 2), b // 2
    y1 = y.reshape(1).astype(jnp.int32)
    z1 = (g // 2).reshape(1).astype(jnp.int32)
    yb = jnp.stack([y, b]).astype(jnp.int32)
    yc = jnp.stack([y, c]).astype(jnp.int32)
    yx = jnp.stack([y, x]).astype(jnp.int32)

    def move(array, axis, target):
        size = lax.axis_size(axis)
        return lax.ppermute(array, axis, [(i, target(i) % size) for i in range(size)])

    def partner(array):
        return move(array, "grid", lambda i: i ^ 1)

    def up(array):
        return move(array, "grid", lambda i: i + 2)

    def down(array):
        return move(array, "grid", lambda i: i - 2)

    def sibling(array):
        return move(array, "band", lambda i: i ^ 1)

    def across(array):
        return move(array, "band", lambda i: i ^ 2)

    field = orbitals.reshape(slab, cells, orb_here)
    rim_rows = 6 * (cells // 4)
    middle, scales, recall = filter_terms(DEGREE)

    def diagonal(array):
        size = peers * bands
        flip = 2 * peers + 1
        return lax.ppermute(array, ("band", "grid"), [(i, i ^ flip) for i in range(size)])

    pot_own = potential.reshape(slab, cells)
    sent0 = call(
        functools.partial(pack_kernel, 0), [f32(3 * cells, LANES)], [y1], [field]
    )[0]
    other0 = partner(sent0)
    dense, part, rim = call(
        dense_kernel,
        [f32(24, 32, cells), f32(19, 16, cells), f32(6, 16, cells)],
        [yc, atom_planes],
        [projectors.transpose(0, 2, 1, 3), pot_own],
        after=[sent0],
    )
    part = partner(part)
    rim_a = move(rim, "grid", lambda i: i + 2 if i % 2 else i - 2)
    rim_b = move(rim, "grid", lambda i: i + 1 if i % 2 else i - 1)
    sent1 = call(
        functools.partial(pack_kernel, 1),
        [f32(3 * cells, LANES)],
        [y1],
        [field],
        after=[other0],
    )[0]
    other1 = partner(sent1)
    pot_part = part
    part = call(
        gather_kernel, [f32(30, 16, cells)], [y1], [part, rim_a, rim_b], after=[sent1]
    )[0]
    mh, ml, th, tl = call(
        maps_kernel,
        [bf16(6, 256, cells)] * 2 + [bf16(6, cells, 256)] * 2,
        [yc],
        [dense, part, sibling(part)],
    )
    pot = call(
        functools.partial(potential_kernel, -(middle + 0.5 * WEIGHTS[0])),
        [bf16(cells, LANES)],
        [y1],
        [pot_own, pot_part],
        after=[mh],
    )[0]
    kb = jnp.broadcast_to(jnp.tile(kb_energy, 4)[:, None], (32, LANES))
    ch, cl = (jnp.asarray(m) for m in plane_matrix(ny, nz))

    chunks = []
    for k, got in enumerate((other0, other1)):
        made = call(
            functools.partial(assemble_kernel, k),
            [f32(6, cells, LANES)] + [f32(rim_rows + 16, LANES)] * 2 + [f32(32, LANES)],
            [y1],
            [field, got, mh, ml],
            after=[pot] if k else [],
        )
        chunks.append(
            dict(v=made[0], prev=None, below=up(made[1]), above=down(made[2]), coef=made[3])
        )

    for level in range(DEGREE):
        first, last = level == 0, level == DEGREE - 1
        for s in chunks:
            arrays = [s["v"]] + ([] if first else [s["prev"]]) + [s["below"], s["above"]]
            arrays += [s["coef"], kb, ch, cl, th, tl, pot]
            if last:
                out = [f32(rim_rows, LANES)] * 4
            else:
                arrays += [mh, ml]
                out = [f32(6, cells, LANES)] + [f32(rim_rows + 16, LANES)] * 2 + [f32(32, LANES)]
            made = call(
                functools.partial(level_kernel, scales[level], recall[level], first, last),
                out,
                [yx] if last else [],
                arrays,
                [pltpu.VMEM((18, cells, LANES), F32)],
                cost=1 << 29,
            )
            if last:
                own, for_y, for_x, rest = made
                s["pieces"] = [own, across(for_x), partner(for_y), diagonal(rest)]
                s["for_x"], s["rest"] = for_x, rest
            else:
                s["prev"], s["v"] = s["v"], made[0]
                s["coef"], s["below"], s["above"] = made[3], up(made[1]), down(made[2])

    tile0, rest = call(
        tile_kernel,
        [f32(4 * rim_rows, LANES), f32(2 * rim_rows, LANES)],
        [y1],
        chunks[0]["pieces"] + [s["rest"] for s in chunks],
    )
    tile1 = call(tile_kernel, [f32(4 * rim_rows, LANES)], [y1], chunks[1]["pieces"])[0]
    early = call(
        gram_early_kernel, [f32(256, 384)], [], [tile0, tile1, sibling(tile0)]
    )[0]
    quarters = call(
        gram_kernel,
        [f32(64, bands * 128)] * 4,
        [y1],
        [tile0, tile1, sibling(tile1), early],
        [pltpu.VMEM((4, 64, bands * 128), F32)],
    )
    partial = call(
        add_kernel,
        [f32(64, bands * 128)],
        [],
        [quarters[0], partner(quarters[1]), across(quarters[2]), diagonal(quarters[3])],
    )[0]
    rest, partial = lax.optimization_barrier((rest, partial))
    rest = partner(rest)
    factor = 1.0 / (slab * cells * peers)
    pairs = peers // 2
    if pairs <= 4:
        moved = [partial]
        for k in range(1, pairs):
            moved.append(move(partial, "grid", lambda i, k=k: i + 2 * k))
        total = call(
            functools.partial(ring_add_kernel, factor),
            [f32(64, bands * 128)],
            [z1],
            moved,
            [pltpu.VMEM((pairs, 64, bands * 128), F32)],
            after=[rest],
        )[0]
    else:
        groups = [[2 * i + j for i in range(pairs)] for j in range(2)]
        total = lax.psum(partial, "grid", axis_index_groups=groups)
        total = call(
            functools.partial(scale_kernel, factor), [f32(64, bands * 128)], [], [total]
        )[0]
    gram = call(
        order_kernel,
        [jax.ShapeDtypeStruct((128, bands * 128), F32)],
        [yb],
        [total, partner(total)],
    )[0]
    filtered = call(
        unpack_kernel,
        [jax.ShapeDtypeStruct((slab, cells, LANES), F32)],
        [yx],
        [s["pieces"][0] for s in chunks]
        + [s["for_x"] for s in chunks]
        + [s["pieces"][2] for s in chunks]
        + [rest],
    )[0]
    return (filtered.reshape(orbitals.shape), gram)


def solution(mesh):
    return jax.shard_map(
        shards,
        mesh=mesh,
        in_specs=(
            P("grid", None, None, "band"),
            P("grid", None, None),
            P("grid", None, None, None),
            P("grid", None),
            P(),
        ),
        out_specs=(P("grid", None, None, "band"), P("band", None)),
        check_vma=False,
    )
```
